256 devices in a mesh: row: 16 (over z_hi, x), col: 16 (over z_lo, y, core).
Axes of the slice: x: 4, y: 4, z: 8 (z_hi: 4, z_lo: 2; z = z_hi * 2 + z_lo), core: 2. Of those that a mesh axis runs over, the one named last changes fastest.
Arguments:
- pair: bfloat16 [512, 512, 128], P('row', 'col'), may hold values from -6 to 6
- pair_mask: int32 [512, 512], P('row', 'col'), may hold values 0 or 1
- proj_weight: bfloat16 [2, 128, 512], replicated, may hold values from -0.5 to 0.5
- gate_weight: bfloat16 [2, 128, 128], replicated, may hold values from -0.5 to 0.5
- out_weight: bfloat16 [2, 128, 128], replicated, may hold values from -0.5 to 0.5
- in_gain: float32 [2, 128], replicated, may hold values from 0.1 to 1.9
- in_bias: float32 [2, 128], replicated, may hold values from -3 to 3
- mid_gain: float32 [2, 128], replicated, may hold values from 0.1 to 1.9
- mid_bias: float32 [2, 128], replicated, may hold values from -3 to 3
Outputs:
- updated: bfloat16 [512, 512, 128], P('row', 'col')
The draws below stay inside these ranges and needn't reach their ends.
All inputs are finite; a program needn't handle non-finite values. No bound on the sum of `pair_mask` on one device may be relied on, other than what follows from the above.
Results may differ from the reference program's by a relative error of at most 0.017.
Values may be sent and summed in bfloat16 or wider, within the bound.
No kernel may reach another device: no remote copies, remote signals or barrier semaphores. Data moves between devices by JAX's collectives and lax.ppermute only.
A program may use at most 128 MiB of HBM per device.

```python
import jax
import jax.numpy as jnp
from jax import lax

C = 128
HID = 128
TOKENS = 512


def touch_ends(entries, key, least, top_value):
    index_at = [jax.random.randint(jax.random.fold_in(key, axis), (), 0, length) for axis, length in enumerate(entries.shape)]
    main_axis = entries.shape.index(max(entries.shape))
    neighbour = index_at[:main_axis] + [(index_at[main_axis] + 1) % entries.shape[main_axis]] + index_at[main_axis + 1:]
    return entries.at[tuple(index_at)].set(least).at[tuple(neighbour)].set(top_value)


def steps_of(rng, shape, pieces, least, top_value):
    level, own = 1.0, jax.random.fold_in(rng, 6)
    for position, shards_of in pieces:
        steps = jnp.exp(jax.random.uniform(jax.random.fold_in(own, position), (shards_of,), jnp.float32, least / len(pieces), top_value / len(pieces)))
        level = level * jnp.repeat(steps, shape[position] // shards_of).reshape([-1 if axis == position else 1 for axis in range(len(shape))])
    return level


def centred(key, extent, spread, limit, cuts=(), dtype=jnp.bfloat16):
    drawn = jax.random.normal(key, extent, jnp.float32) * spread
    if len(cuts) > 0:
        drawn = steps_of(key, extent, cuts, -0.22, 0.18) * drawn
    return jnp.clip(drawn, min=-limit, max=limit).astype(dtype)


def setup_inputs(seed: int = 0) -> dict:
    arg_keys = jax.random.split(jax.random.key(seed), 10)
    pair = centred(arg_keys[0], (TOKENS, TOKENS, C), 1.0, 6.0, ((0, 16), (1, 16)))
    pair_mask = touch_ends((jax.random.randint(arg_keys[1], (TOKENS, TOKENS), 0, 8) < 7).astype(jnp.int32), jax.random.fold_in(arg_keys[1], 1), 0, 1)
    proj_weight = centred(arg_keys[2], (2, C, 4 * HID), C ** -0.5, 0.5)
    gate_weight = centred(arg_keys[3], (2, C, C), C ** -0.5, 0.5)
    out_weight = centred(arg_keys[4], (2, HID, C), HID ** -0.5, 0.5)
    in_gain = jnp.clip(1.0 + 0.18 * jax.random.normal(arg_keys[5], (2, C), jnp.float32), 0.1, 1.9)
    in_bias = centred(arg_keys[6], (2, C), 0.5, 3.0, (), jnp.float32)
    mid_gain = jnp.clip(1.0 + 0.18 * jax.random.normal(arg_keys[7], (2, HID), jnp.float32), 0.1, 1.9)
    mid_bias = centred(arg_keys[8], (2, HID), 0.5, 3.0, (), jnp.float32)
    return dict(pair=pair, pair_mask=pair_mask, proj_weight=proj_weight, gate_weight=gate_weight, out_weight=out_weight, in_gain=in_gain, in_bias=in_bias, mid_gain=mid_gain, mid_bias=mid_bias)


def layer_norm(values, gain, bias):
    mean = lax.optimization_barrier(jnp.mean(values, axis=-1, keepdims=True))
    centered = values - mean
    var = lax.optimization_barrier(jnp.mean(centered * centered, axis=-1, keepdims=True))
    return centered / jnp.sqrt(var + 1e-05) * gain + bias

def one_pass(state, pair_mask, proj_w, gate_w, out_w, gain_in, bias_in, gain_mid, bias_mid, incoming):
    size = state.shape[0]
    normed = layer_norm(state.astype(jnp.float32), gain_in, bias_in).astype(jnp.bfloat16)
    flat = normed.reshape(size * size, C)
    proj = jnp.dot(flat, proj_w, preferred_element_type=jnp.float32).reshape(size, size, 4 * HID)
    maskf = pair_mask.astype(jnp.float32)[:, :, None]
    left = (maskf * jax.nn.sigmoid(proj[:, :, :HID]) * proj[:, :, HID:2 * HID]).astype(jnp.bfloat16)
    right = (maskf * jax.nn.sigmoid(proj[:, :, 2 * HID:3 * HID]) * proj[:, :, 3 * HID:]).astype(jnp.bfloat16)
    gate = jax.nn.sigmoid(jnp.dot(flat, gate_w, preferred_element_type=jnp.float32))
    lf = left.astype(jnp.float32)
    rf = right.astype(jnp.float32)
    if incoming:
        tri = jnp.einsum('kic,kjc->ijc', lf, rf)
    else:
        tri = jnp.einsum('ikc,jkc->ijc', lf, rf)
    tri_normed = layer_norm(tri, gain_mid, bias_mid).astype(jnp.bfloat16).reshape(size * size, HID)
    update = gate * jnp.dot(tri_normed, out_w, preferred_element_type=jnp.float32)
    return (state.astype(jnp.float32) + update.reshape(size, size, C)).astype(jnp.bfloat16)

def reference(pair, pair_mask, proj_weight, gate_weight, out_weight, in_gain, in_bias, mid_gain, mid_bias):
    state = pair
    for step in range(2):
        state = one_pass(state, pair_mask, proj_weight[step], gate_weight[step], out_weight[step], in_gain[step], in_bias[step], mid_gain[step], mid_bias[step], step == 1)
    return state
```

```python
import jax
import jax.numpy as jnp
from jax import lax
from jax.experimental import pallas as pl
from jax.experimental.pallas import tpu as pltpu
from jax.sharding import Mesh
from jax.sharding import PartitionSpec as P

F32 = jnp.float32
BF16 = jnp.bfloat16
CHIPS = ("zh", "x", "zl", "y")
VMEM_LIMIT = 48 * 1024 * 1024


def dot(a, b, dims):
    return lax.dot_general(a, b, (dims, ((), ())), preferred_element_type=F32)


def sigmoid(v):
    return 0.5 * jnp.tanh(0.5 * v) + 0.5


def columns(gains, scr):
    for n, ref in enumerate(gains):
        scr[2 * n : 2 * n + 2, :] = ref[...]
    return scr[...].T


def norm_channels(v, gain, bias):
    mean = jnp.mean(v, axis=0, keepdims=True)
    centered = v - mean
    var = jnp.mean(centered * centered, axis=0, keepdims=True)
    return centered * lax.rsqrt(var + 1e-05) * gain + bias


def swap_groups(v):
    lane = lax.broadcasted_iota(jnp.int32, v[0].shape, v[0].ndim - 1)
    low = lane < 64
    even = (lane // 32) % 2 == 0
    axis = v[0].ndim - 1

    def exchange(a, b, keep, up, down):
        return jnp.where(keep, a, pltpu.roll(b, up, axis)), jnp.where(keep, pltpu.roll(a, down, axis), b)

    a0, a2 = exchange(v[0], v[2], low, 64, 64)
    a1, a3 = exchange(v[1], v[3], low, 64, 64)
    b0, b1 = exchange(a0, a1, even, 32, 96)
    b2, b3 = exchange(a2, a3, even, 32, 96)
    return [b0, b1, b2, b3]


def project(normed, w_t, mask, a, scr):
    proj = dot(w_t, normed, ((1,), (0,)))
    hid = proj.shape[0] // 4
    row = mask[a : a + 1, :]
    left = row * sigmoid(proj[:hid]) * proj[hid : 2 * hid]
    right = row * sigmoid(proj[2 * hid : 3 * hid]) * proj[3 * hid :]
    scr[pl.ds(a, hid, stride=16), :] = left
    scr[pl.ds(a + 8, hid, stride=16), :] = right


def begin_kernel(pair, mask, proj_w, ig, ib, mg, mb, sent, pair_t, normed_t, mask_out, cols, scr, gains):
    col = columns((ig, ib, mg, mb), gains)
    cols[...] = col
    m = mask[...].astype(F32)
    m8 = jnp.concatenate([m[8 * q : 8 * q + 8] for q in range(4)], axis=1)
    mask_out[...] = m8
    w_t = proj_w[0].astype(F32).T.astype(BF16)
    for a in range(8):
        block = jnp.concatenate([pair[8 * q + a] for q in range(4)], axis=0).astype(F32).T
        lanes = slice(128 * a, 128 * a + 128)
        pair_t[:, lanes] = block.astype(BF16)
        normed = norm_channels(block, col[:, 0:1], col[:, 2:3]).astype(BF16)
        normed_t[:, lanes] = normed
        project(normed, w_t, m8, a, scr)
    sent[...] = scr[...].astype(BF16)


def update(tri, state_t, normed_t, gate_wt, out_wt, gain, bias, a, mean, rstd):
    lanes = slice(128 * a, 128 * a + 128)
    chans = state_t.shape[0]
    v = tri[pl.ds(a, chans, stride=8), :]
    v = ((v - mean[a : a + 1]) * rstd[a : a + 1] * gain + bias).astype(BF16)
    gate = sigmoid(dot(gate_wt, normed_t[:, lanes], ((1,), (0,))))
    return state_t[:, lanes].astype(F32) + gate * dot(out_wt, v, ((1,), (0,)))


def statistics(got, tri):
    v = got[...].astype(F32)
    tri[...] = v
    v = v.reshape(-1, 8, 128)
    mean = jnp.mean(v, axis=0)
    centered = v - mean[None]
    return mean, lax.rsqrt(jnp.mean(centered * centered, axis=0) + 1e-05)


def middle_kernel(got, pair_t, normed_t, mask, cols, proj_w, gate_w, out_w, sent, state_out, normed_out, tri, scr):
    col = cols[...]
    w_t = proj_w[1].astype(F32).T.astype(BF16)
    gate_wt = gate_w[0].astype(F32).T.astype(BF16)
    out_wt = out_w[0].astype(F32).T.astype(BF16)
    mean, rstd = statistics(got, tri)
    m8 = mask[...]
    for a in range(8):
        lanes = slice(128 * a, 128 * a + 128)
        state = update(tri, pair_t, normed_t, gate_wt, out_wt, col[:, 4:5], col[:, 6:7], a, mean, rstd).astype(BF16)
        state_out[:, lanes] = state
        normed = norm_channels(state.astype(F32), col[:, 1:2], col[:, 3:4]).astype(BF16)
        normed_out[:, lanes] = normed
        project(normed, w_t, m8, a, scr)
    sent[...] = scr[...].astype(BF16)


def end_kernel(got, state_t, normed_t, cols, gate_w, out_w, out, tri):
    col = cols[...]
    gate_wt = gate_w[1].astype(F32).T.astype(BF16)
    out_wt = out_w[1].astype(F32).T.astype(BF16)
    mean, rstd = statistics(got, tri)
    for a in range(8):
        state = update(tri, state_t, normed_t, gate_wt, out_wt, col[:, 5:6], col[:, 7:8], a, mean, rstd).T.astype(BF16)
        for q in range(4):
            out[8 * q + a] = state[32 * q : 32 * q + 32]


def gather_groups(got, rows, left, right):
    v = got[...].astype(F32).reshape(16, 8, rows, 128)
    for h in range(2):
        lanes = slice(128 * h, 128 * h + 128)
        for q, t in enumerate(swap_groups([v[:, 4 * h + g] for g in range(4)])):
            left[:, q, :, lanes] = t[:, :8]
            if right is not None:
                right[:, q, :, lanes] = t[:, 8:]


def scatter_groups(prod, store):
    v = prod.reshape(-1, 4, 8, 256)
    for h in range(2):
        lanes = slice(128 * h, 128 * h + 128)
        for g, t in enumerate(swap_groups([v[:, q, :, lanes] for q in range(4)])):
            store(4 * h + g, t)


def outgoing_kernel(got, keep, send, left, right, chunks):
    core = lax.axis_index("core")
    gather_groups(got, 16, left, right)
    lm = left[...].reshape(512, 256).astype(BF16)
    for parity, out in ((1 - core, send), (core, keep)):
        rm = jnp.concatenate([right[2 * n + parity] for n in range(8)], axis=0).reshape(256, 256).astype(BF16)
        prod = dot(lm, rm, ((1,), (1,)))

        def store(c, t):
            chunks[:, c] = t

        scatter_groups(prod, store)
        out[...] = chunks[...].reshape(1024, 128).astype(out.dtype)


def incoming_kernel(got, other, send, left, right, far, chunks):
    core = lax.axis_index("core")
    gather_groups(got, 16, left, right)
    gather_groups(other, 16, far, None)
    rm = right[...].reshape(512, 256).astype(BF16)
    for parity, ref in ((core, left), (1 - core, far)):
        prod = dot(ref[...].reshape(512, 256).astype(BF16), rm, ((0,), (0,)))

        def store(c, t):
            chunks[:, parity, c] = t

        scatter_groups(prod, store)
    send[...] = chunks[...].reshape(1024, 128).astype(BF16)


def call(kernel, outs, scratch):
    return pl.pallas_call(
        kernel,
        out_shape=[jax.ShapeDtypeStruct(shape, dtype) for shape, dtype in outs],
        scratch_shapes=[pltpu.VMEM(shape, F32) for shape in scratch],
        compiler_params=pltpu.CompilerParams(vmem_limit_bytes=VMEM_LIMIT),
    )


def body(pair, mask, proj_w, gate_w, out_w, ig, ib, mg, mb):
    def exchange(v):
        return lax.all_to_all(v, CHIPS, 0, 0, tiled=True)

    def swap(v):
        return lax.ppermute(v, "core", [(0, 1), (1, 0)])

    sent, pair_t, normed_t, m8, cols = call(
        begin_kernel,
        [((2048, 128), BF16), ((128, 1024), BF16), ((128, 1024), BF16), ((8, 128), F32), ((128, 8), F32)],
        [(2048, 128), (8, 128)],
    )(pair, mask, proj_w, ig, ib, mg, mb)
    keep, send = call(
        outgoing_kernel,
        [((1024, 128), F32), ((1024, 128), BF16)],
        [(16, 4, 8, 256), (16, 4, 8, 256), (16, 8, 8, 128)],
    )(exchange(sent))
    got = exchange((keep + swap(send).astype(F32)).astype(BF16))
    sent, state_t, normed_t = call(
        middle_kernel,
        [((2048, 128), BF16), ((128, 1024), BF16), ((128, 1024), BF16)],
        [(1024, 128), (2048, 128)],
    )(got, pair_t, normed_t, m8, cols, proj_w, gate_w, out_w)
    got = exchange(sent)
    (send,) = call(
        incoming_kernel,
        [((1024, 128), BF16)],
        [(16, 4, 8, 256), (16, 4, 8, 256), (16, 4, 8, 256), (8, 2, 8, 8, 128)],
    )(got, swap(got))
    (out,) = call(end_kernel, [((32, 32, 128), BF16)], [(1024, 128)])(
        exchange(send), state_t, normed_t, cols, gate_w, out_w
    )
    return out


def solution(mesh):
    fine = Mesh(mesh.devices.reshape(4, 4, 2, 4, 2), ("zh", "x", "zl", "y", "core"))
    block = P(("zh", "x"), ("zl", "y", "core"))
    return jax.shard_map(
        body,
        mesh=fine,
        in_specs=(block, block, P(), P(), P(), P(), P(), P(), P()),
        out_specs=block,
        check_vma=False,
    )
```

```python
import jax
import jax.numpy as jnp
from jax import lax
from jax.experimental import pallas as pl
from jax.experimental.pallas import tpu as pltpu
from jax.sharding import Mesh
from jax.sharding import PartitionSpec as P

F32 = jnp.float32
BF16 = jnp.bfloat16
CHIPS = ("zh", "x", "zl", "y")
VMEM_LIMIT = 48 * 1024 * 1024
FIRST_LIMIT = 60 * 1024 * 1024


def dot(a, b, dims):
    return lax.dot_general(a, b, (dims, ((), ())), preferred_element_type=F32)


def sigmoid(v):
    return 0.5 * jnp.tanh(0.5 * v) + 0.5


def columns(gains, scr):
    for n, ref in enumerate(gains):
        scr[2 * n : 2 * n + 2, :] = ref[...]
    return scr[...].T


def norm_channels(v, gain, bias):
    mean = jnp.mean(v, axis=0, keepdims=True)
    centered = v - mean
    var = jnp.mean(centered * centered, axis=0, keepdims=True)
    return centered * lax.rsqrt(var + 1e-05) * gain + bias


def swap_groups(v):
    lane = lax.broadcasted_iota(jnp.int32, v[0].shape, v[0].ndim - 1)
    low = lane < 64
    even = (lane // 32) % 2 == 0
    axis = v[0].ndim - 1

    def exchange(a, b, keep, up, down):
        return jnp.where(keep, a, pltpu.roll(b, up, axis)), jnp.where(keep, pltpu.roll(a, down, axis), b)

    a0, a2 = exchange(v[0], v[2], low, 64, 64)
    a1, a3 = exchange(v[1], v[3], low, 64, 64)
    b0, b1 = exchange(a0, a1, even, 32, 96)
    b2, b3 = exchange(a2, a3, even, 32, 96)
    return [b0, b1, b2, b3]


def project(normed, w_t, mask, a, scr):
    proj = dot(w_t, normed, ((1,), (0,)))
    hid = proj.shape[0] // 4
    row = mask[a : a + 1, :]
    left = row * sigmoid(proj[:hid]) * proj[hid : 2 * hid]
    right = row * sigmoid(proj[2 * hid : 3 * hid]) * proj[3 * hid :]
    scr[pl.ds(a, hid, stride=16), :] = left
    scr[pl.ds(a + 8, hid, stride=16), :] = right


def begin_kernel(*refs):
    inputs, (sent, pair_t, normed_t, mask_out, cols) = refs[:7], refs[7:12]
    local, scr, gains, sems = refs[12:19], refs[19], refs[20], refs[21]
    copies = [
        pltpu.make_async_copy(src.at[0] if n == 2 else src, dst, sems.at[n])
        for n, (src, dst) in enumerate(zip(inputs, local))
    ]
    for copy in copies:
        copy.start()
    for copy in copies:
        copy.wait()
    pair, mask, proj_w = local[:3]
    col = columns(local[3:], gains)
    cols[...] = col
    m = mask[...].astype(F32)
    m8 = jnp.concatenate([m[8 * q : 8 * q + 8] for q in range(4)], axis=1)
    mask_out[...] = m8
    w_t = proj_w[...].astype(F32).T.astype(BF16)
    for a in range(8):
        block = jnp.concatenate([pair[8 * q + a] for q in range(4)], axis=0).astype(F32).T
        lanes = slice(128 * a, 128 * a + 128)
        pair_t[:, lanes] = block.astype(BF16)
        normed = norm_channels(block, col[:, 0:1], col[:, 2:3]).astype(BF16)
        normed_t[:, lanes] = normed
        project(normed, w_t, m8, a, scr)
    sent[...] = scr[...].astype(BF16)


def update(tri, state_t, normed_t, gate_wt, out_wt, gain, bias, a, mean, rstd):
    lanes = slice(128 * a, 128 * a + 128)
    chans = state_t.shape[0]
    v = tri[pl.ds(a, chans, stride=8), :]
    v = ((v - mean[a : a + 1]) * rstd[a : a + 1] * gain + bias).astype(BF16)
    gate = sigmoid(dot(gate_wt, normed_t[:, lanes], ((1,), (0,))))
    return state_t[:, lanes].astype(F32) + gate * dot(out_wt, v, ((1,), (0,)))


def statistics(got, tri):
    v = got[...].astype(F32)
    tri[...] = v
    v = v.reshape(-1, 8, 128)
    mean = jnp.mean(v, axis=0)
    centered = v - mean[None]
    return mean, lax.rsqrt(jnp.mean(centered * centered, axis=0) + 1e-05)


def middle_kernel(got, pair_t, normed_t, mask, cols, proj_w, gate_w, out_w, sent, state_out, normed_out, tri, scr):
    col = cols[...]
    w_t = proj_w[1].astype(F32).T.astype(BF16)
    gate_wt = gate_w[0].astype(F32).T.astype(BF16)
    out_wt = out_w[0].astype(F32).T.astype(BF16)
    mean, rstd = statistics(got, tri)
    m8 = mask[...]
    for a in range(8):
        lanes = slice(128 * a, 128 * a + 128)
        state = update(tri, pair_t, normed_t, gate_wt, out_wt, col[:, 4:5], col[:, 6:7], a, mean, rstd).astype(BF16)
        state_out[:, lanes] = state
        normed = norm_channels(state.astype(F32), col[:, 1:2], col[:, 3:4]).astype(BF16)
        normed_out[:, lanes] = normed
        project(normed, w_t, m8, a, scr)
    sent[...] = scr[...].astype(BF16)


def end_kernel(got, state_t, normed_t, cols, gate_w, out_w, out, tri):
    col = cols[...]
    gate_wt = gate_w[1].astype(F32).T.astype(BF16)
    out_wt = out_w[1].astype(F32).T.astype(BF16)
    mean, rstd = statistics(got, tri)
    for a in range(8):
        state = update(tri, state_t, normed_t, gate_wt, out_wt, col[:, 5:6], col[:, 7:8], a, mean, rstd).T.astype(BF16)
        for q in range(4):
            out[8 * q + a] = state[32 * q : 32 * q + 32]


def gather_groups(got, rows, left, right):
    v = got[...].astype(F32).reshape(16, 8, rows, 128)
    for h in range(2):
        lanes = slice(128 * h, 128 * h + 128)
        for q, t in enumerate(swap_groups([v[:, 4 * h + g] for g in range(4)])):
            left[:, q, :, lanes] = t[:, :8]
            if right is not None:
                right[:, q, :, lanes] = t[:, 8:]


def scatter_groups(prod, store):
    v = prod.reshape(-1, 4, 8, 256)
    for h in range(2):
        lanes = slice(128 * h, 128 * h + 128)
        for g, t in enumerate(swap_groups([v[:, q, :, lanes] for q in range(4)])):
            store(4 * h + g, t)


def outgoing_kernel(got, keep, send, left, right, chunks):
    core = lax.axis_index("core")
    gather_groups(got, 16, left, right)
    lm = left[...].reshape(512, 256).astype(BF16)
    for parity, out in ((1 - core, send), (core, keep)):
        rm = jnp.concatenate([right[2 * n + parity] for n in range(8)], axis=0).reshape(256, 256).astype(BF16)
        prod = dot(lm, rm, ((1,), (1,)))

        def store(c, t):
            chunks[:, c] = t

        scatter_groups(prod, store)
        out[...] = chunks[...].reshape(1024, 128).astype(out.dtype)


def incoming_kernel(got, other, send, left, right, far, chunks):
    core = lax.axis_index("core")
    gather_groups(got, 16, left, right)
    gather_groups(other, 16, far, None)
    rm = right[...].reshape(512, 256).astype(BF16)
    for parity, ref in ((core, left), (1 - core, far)):
        prod = dot(ref[...].reshape(512, 256).astype(BF16), rm, ((0,), (0,)))

        def store(c, t):
            chunks[:, parity, c] = t

        scatter_groups(prod, store)
    send[...] = chunks[...].reshape(1024, 128).astype(BF16)


def call(kernel, outs, scratch):
    return pl.pallas_call(
        kernel,
        out_shape=[jax.ShapeDtypeStruct(shape, dtype) for shape, dtype in outs],
        scratch_shapes=[pltpu.VMEM(shape, F32) for shape in scratch],
        compiler_params=pltpu.CompilerParams(vmem_limit_bytes=VMEM_LIMIT),
    )


def body(pair, mask, proj_w, gate_w, out_w, ig, ib, mg, mb):
    def exchange(v):
        return lax.all_to_all(v, CHIPS, 0, 0, tiled=True)

    def swap(v):
        return lax.ppermute(v, "core", [(0, 1), (1, 0)])

    first = (pair, mask, proj_w, ig, ib, mg, mb)
    sent, pair_t, normed_t, m8, cols = pl.pallas_call(
        begin_kernel,
        in_specs=[pl.BlockSpec(memory_space=pl.ANY)] * 7,
        out_shape=[
            jax.ShapeDtypeStruct((2048, 128), BF16),
            jax.ShapeDtypeStruct((128, 1024), BF16),
            jax.ShapeDtypeStruct((128, 1024), BF16),
            jax.ShapeDtypeStruct((8, 128), F32),
            jax.ShapeDtypeStruct((128, 8), F32),
        ],
        scratch_shapes=[pltpu.VMEM(v.shape[1:] if v is proj_w else v.shape, v.dtype) for v in first]
        + [pltpu.VMEM((2048, 128), F32), pltpu.VMEM((8, 128), F32), pltpu.SemaphoreType.DMA((7,))],
        compiler_params=pltpu.CompilerParams(vmem_limit_bytes=FIRST_LIMIT),
    )(*first)
    keep, send = call(
        outgoing_kernel,
        [((1024, 128), F32), ((1024, 128), BF16)],
        [(16, 4, 8, 256), (16, 4, 8, 256), (16, 8, 8, 128)],
    )(exchange(sent))
    got = exchange((keep + swap(send).astype(F32)).astype(BF16))
    sent, state_t, normed_t = call(
        middle_kernel,
        [((2048, 128), BF16), ((128, 1024), BF16), ((128, 1024), BF16)],
        [(1024, 128), (2048, 128)],
    )(got, pair_t, normed_t, m8, cols, proj_w, gate_w, out_w)
    got = exchange(sent)
    (send,) = call(
        incoming_kernel,
        [((1024, 128), BF16)],
        [(16, 4, 8, 256), (16, 4, 8, 256), (16, 4, 8, 256), (8, 2, 8, 8, 128)],
    )(got, swap(got))
    (out,) = call(end_kernel, [((32, 32, 128), BF16)], [(1024, 128)])(
        exchange(send), state_t, normed_t, cols, gate_w, out_w
    )
    return out


def solution(mesh):
    fine = Mesh(mesh.devices.reshape(4, 4, 2, 4, 2), ("zh", "x", "zl", "y", "core"))
    block = P(("zh", "x"), ("zl", "y", "core"))
    return jax.shard_map(
        body,
        mesh=fine,
        in_specs=(block, block, P(), P(), P(), P(), P(), P(), P()),
        out_specs=block,
        check_vma=False,
    )
```

```python
import jax
import jax.numpy as jnp
from jax import lax
from jax.experimental import pallas as pl
from jax.experimental.pallas import tpu as pltpu
from jax.sharding import Mesh
from jax.sharding import PartitionSpec as P

F32 = jnp.float32
BF16 = jnp.bfloat16
CHIPS = ("zh", "x", "zl", "y")
VMEM_LIMIT = 48 * 1024 * 1024


def dot(a, b, dims):
    return lax.dot_general(a, b, (dims, ((), ())), preferred_element_type=F32)


def sigmoid(v):
    return 0.5 * jnp.tanh(0.5 * v) + 0.5


def columns(gains, scr):
    for n, ref in enumerate(gains):
        scr[2 * n : 2 * n + 2, :] = ref[...]
    return scr[...].T


def norm_channels(v, gain, bias):
    mean = jnp.mean(v, axis=0, keepdims=True)
    centered = v - mean
    var = jnp.mean(centered * centered, axis=0, keepdims=True)
    return centered * lax.rsqrt(var + 1e-05) * gain + bias


def swap_groups(v):
    lane = lax.broadcasted_iota(jnp.int32, v[0].shape, v[0].ndim - 1)
    low = lane < 64
    even = (lane // 32) % 2 == 0
    axis = v[0].ndim - 1

    def exchange(a, b, keep, up, down):
        return jnp.where(keep, a, pltpu.roll(b, up, axis)), jnp.where(keep, pltpu.roll(a, down, axis), b)

    a0, a2 = exchange(v[0], v[2], low, 64, 64)
    a1, a3 = exchange(v[1], v[3], low, 64, 64)
    b0, b1 = exchange(a0, a1, even, 32, 96)
    b2, b3 = exchange(a2, a3, even, 32, 96)
    return [b0, b1, b2, b3]


def first_mask(mask):
    m = mask[...].astype(F32)
    return jnp.concatenate([m[8 * q : 8 * q + 8] for q in range(4)], axis=1)


def transposed(w):
    return w.astype(F32).T.astype(BF16)


def lanes_of(a):
    return slice(128 * a, 128 * a + 128)


def gated(proj, mask, scr):
    hid = proj.shape[0] // 4
    for a in range(8):
        lanes = lanes_of(a)
        row = mask[a : a + 1, :]
        left = row * sigmoid(proj[:hid, lanes]) * proj[hid : 2 * hid, lanes]
        right = row * sigmoid(proj[2 * hid : 3 * hid, lanes]) * proj[3 * hid :, lanes]
        scr[pl.ds(a, hid, stride=16), :] = left
        scr[pl.ds(a + 8, hid, stride=16), :] = right


def begin_kernel(*refs):
    inputs, (sent, pair_t, normed_t, mask_out, cols) = refs[:7], refs[7:12]
    local, (scr, gains, proj, sems) = refs[12:19], refs[19:]
    parts = [(inputs[0].at[8 * n : 8 * n + 8], local[0].at[8 * n : 8 * n + 8]) for n in range(4)]
    parts += [(inputs[2].at[0], local[2]), (inputs[1], local[1])] + list(zip(inputs[3:], local[3:]))
    copies = [pltpu.make_async_copy(src, dst, sems.at[n]) for n, (src, dst) in enumerate(parts)]
    for copy in copies:
        copy.start()
    for copy in copies:
        copy.wait()
    pair, mask, proj_w = local[:3]
    col = columns(local[3:], gains)
    cols[...] = col
    m8 = first_mask(mask)
    mask_out[...] = m8
    w_t = transposed(proj_w[...])
    for a in range(8):
        block = jnp.concatenate([pair[8 * q + a] for q in range(4)], axis=0).astype(F32).T
        pair_t[:, lanes_of(a)] = block.astype(BF16)
        normed_t[:, lanes_of(a)] = norm_channels(block, col[:, 0:1], col[:, 2:3]).astype(BF16)
    proj[...] = dot(w_t, normed_t[...], ((1,), (0,)))
    gated(proj, m8, scr)
    sent[...] = scr[...].astype(BF16)


def statistics(got, tri):
    v = got[...].astype(F32)
    tri[...] = v
    v = v.reshape(8, 16, 8, 128)
    mean = jnp.mean(jnp.mean(v, axis=1), axis=0)
    centered = v - mean[None, None]
    return mean, lax.rsqrt(jnp.mean(jnp.mean(centered * centered, axis=1), axis=0) + 1e-05)


def norm_chunks(got, tri, gain, bias, out):
    mean, rstd = statistics(got, tri)
    chans = out.shape[0]
    for a in range(8):
        v = tri[pl.ds(a, chans, stride=8), :]
        out[:, lanes_of(a)] = ((v - mean[a : a + 1]) * rstd[a : a + 1] * gain + bias).astype(BF16)


def middle_kernel(got, pair_t, gate, mask, cols, w_t, out_t, sent, state_out, normed_out, tri, scr, proj, upd, tn):
    col = cols[...]
    norm_chunks(got, tri, col[:, 4:5], col[:, 6:7], tn)
    upd[...] = dot(out_t[...], tn[...], ((1,), (0,)))
    for a in range(8):
        lanes = lanes_of(a)
        state = (pair_t[:, lanes].astype(F32) + gate[:, lanes] * upd[:, lanes]).astype(BF16)
        state_out[:, lanes] = state
        normed_out[:, lanes] = norm_channels(state.astype(F32), col[:, 1:2], col[:, 3:4]).astype(BF16)
    proj[...] = dot(w_t[...], normed_out[...], ((1,), (0,)))
    gated(proj, mask[...], scr)
    sent[...] = scr[...].astype(BF16)


def end_kernel(got, state_t, gate, cols, out_t, out, tri, upd, tn):
    col = cols[...]
    norm_chunks(got, tri, col[:, 5:6], col[:, 7:8], tn)
    upd[...] = dot(out_t[...], tn[...], ((1,), (0,)))
    for a in range(8):
        lanes = lanes_of(a)
        state = (state_t[:, lanes].astype(F32) + gate[:, lanes] * upd[:, lanes]).T.astype(BF16)
        out[:, a] = state.reshape(4, 32, 128)


def gather_groups(got, rows, left, right):
    v = got[...].astype(F32).reshape(16, 8, rows, 128)
    for h in range(2):
        lanes = slice(128 * h, 128 * h + 128)
        for q, t in enumerate(swap_groups([v[:, 4 * h + g] for g in range(4)])):
            left[:, q, :, lanes] = t[:, :8]
            if right is not None:
                right[:, q, :, lanes] = t[:, 8:]


def scatter_groups(prod, store):
    v = prod.reshape(-1, 4, 8, 256)
    for h in range(2):
        lanes = slice(128 * h, 128 * h + 128)
        for g, t in enumerate(swap_groups([v[:, q, :, lanes] for q in range(4)])):
            store(4 * h + g, t)


def outgoing_chunks(lm, rm, chunks):
    prod = dot(lm, rm, ((1,), (1,)))

    def store(c, t):
        chunks[:, c] = t

    scatter_groups(prod, store)
    return chunks[...].reshape(1024, 128)


def outgoing_send_kernel(got, send, lm, rm, left, right, chunks):
    core = lax.axis_index("core")
    gather_groups(got, 16, left, right)
    lm[...] = left[...].reshape(512, 256).astype(BF16)

    def half(parity):
        return jnp.concatenate([right[2 * n + parity] for n in range(8)], axis=0).reshape(256, 256).astype(BF16)

    rm[...] = half(core)
    send[...] = outgoing_chunks(lm[...], half(1 - core), chunks).astype(BF16)


def outgoing_keep_kernel(lm, rm, normed_t, proj_w, gate_w, out_w, keep, gate, w_t, out_t, chunks):
    keep[...] = outgoing_chunks(lm[...], rm[...], chunks)
    gate[...] = sigmoid(dot(transposed(gate_w[0]), normed_t[...], ((1,), (0,))))
    w_t[...] = transposed(proj_w[1])
    out_t[...] = transposed(out_w[0])


def incoming_chunks(left, rm, store):
    scatter_groups(dot(left[...].reshape(512, 256).astype(BF16), rm, ((0,), (0,))), store)


def incoming_near_kernel(got, normed_t, gate_w, out_w, near, rm, gate, out_t, left, right):
    gather_groups(got, 16, left, right)
    rm[...] = right[...].reshape(512, 256).astype(BF16)

    def store(c, t):
        near[:, c] = t

    incoming_chunks(left, rm[...], store)
    gate[...] = sigmoid(dot(transposed(gate_w[1]), normed_t[...], ((1,), (0,))))
    out_t[...] = transposed(out_w[1])


def incoming_far_kernel(other, rm, near, send, left, chunks):
    core = lax.axis_index("core")
    chunks[:, core] = near[...]
    gather_groups(other, 16, left, None)

    def store(c, t):
        chunks[:, 1 - core, c] = t

    incoming_chunks(left, rm[...], store)
    send[...] = chunks[...].reshape(1024, 128).astype(BF16)


def call(kernel, outs, scratch, flops=0):
    return pl.pallas_call(
        kernel,
        out_shape=[jax.ShapeDtypeStruct(shape, dtype) for shape, dtype in outs],
        scratch_shapes=[pltpu.VMEM(shape, dtype) for shape, dtype in scratch],
        compiler_params=pltpu.CompilerParams(vmem_limit_bytes=VMEM_LIMIT),
        cost_estimate=pl.CostEstimate(flops=flops, bytes_accessed=1 << 20, transcendentals=1 << 17) if flops else None,
    )


def body(pair, mask, proj_w, gate_w, out_w, ig, ib, mg, mb):
    def exchange(v):
        return lax.all_to_all(v, CHIPS, 0, 0, tiled=True)

    def swap(v):
        return lax.ppermute(v, "core", [(0, 1), (1, 0)])

    first = (pair, mask, proj_w, ig, ib, mg, mb)
    sent, pair_t, normed_t, m8, cols = pl.pallas_call(
        begin_kernel,
        in_specs=[pl.BlockSpec(memory_space=pl.ANY)] * 7,
        out_shape=[
            jax.ShapeDtypeStruct((2048, 128), BF16),
            jax.ShapeDtypeStruct((128, 1024), BF16),
            jax.ShapeDtypeStruct((128, 1024), BF16),
            jax.ShapeDtypeStruct((8, 128), F32),
            jax.ShapeDtypeStruct((128, 8), F32),
        ],
        scratch_shapes=[pltpu.VMEM(v.shape[1:] if v is proj_w else v.shape, v.dtype) for v in first]
        + [
            pltpu.VMEM((2048, 128), F32),
            pltpu.VMEM((8, 128), F32),
            pltpu.VMEM((512, 1024), F32),
            pltpu.SemaphoreType.DMA((10,)),
        ],
        compiler_params=pltpu.CompilerParams(vmem_limit_bytes=VMEM_LIMIT),
    )(*(pltpu.with_memory_space_constraint(v, pltpu.HBM) for v in first))
    wide = (128, 1024)
    square = (16, 4, 8, 256)
    send, lm, rm = call(
        outgoing_send_kernel,
        [((1024, 128), BF16), ((512, 256), BF16), ((256, 256), BF16)],
        [(square, F32), (square, F32), ((16, 8, 8, 128), F32)],
    )(exchange(sent))
    far = swap(send)
    keep, gate, w_t, out_t = call(
        outgoing_keep_kernel,
        [((1024, 128), F32), (wide, F32), ((512, 128), BF16), ((128, 128), BF16)],
        [((16, 8, 8, 128), F32)],
        1 << 28,
    )(lm, rm, normed_t, proj_w, gate_w, out_w)
    got = exchange((keep + far.astype(F32)).astype(BF16))
    sent, state_t, normed_t = call(
        middle_kernel,
        [((2048, 128), BF16), (wide, BF16), (wide, BF16)],
        [((1024, 128), F32), ((2048, 128), F32), ((512, 1024), F32), (wide, F32), (wide, BF16)],
    )(got, pair_t, gate, m8, cols, w_t, out_t)
    got = exchange(sent)
    far = swap(got)
    near, rm, gate, out_t = call(
        incoming_near_kernel,
        [((8, 8, 8, 128), F32), ((512, 256), BF16), (wide, F32), ((128, 128), BF16)],
        [(square, F32), (square, F32)],
        1 << 28,
    )(got, normed_t, gate_w, out_w)
    (send,) = call(
        incoming_far_kernel,
        [((1024, 128), BF16)],
        [(square, F32), ((8, 2, 8, 8, 128), F32)],
    )(far, rm, near)
    (out,) = call(
        end_kernel,
        [((4, 8, 32, 128), BF16)],
        [((1024, 128), F32), (wide, F32), (wide, BF16)],
    )(exchange(send), state_t, gate, cols, out_t)
    return out.reshape(32, 32, 128)


def solution(mesh):
    fine = Mesh(mesh.devices.reshape(4, 4, 2, 4, 2), ("zh", "x", "zl", "y", "core"))
    block = P(("zh", "x"), ("zl", "y", "core"))
    return jax.shard_map(
        body,
        mesh=fine,
        in_specs=(block, block, P(), P(), P(), P(), P(), P(), P()),
        out_specs=block,
        check_vma=False,
    )
```

```python
import jax
import jax.numpy as jnp
from jax import lax
from jax.experimental import pallas as pl
from jax.experimental.pallas import tpu as pltpu
from jax.sharding import Mesh
from jax.sharding import PartitionSpec as P

F32 = jnp.float32
BF16 = jnp.bfloat16
CHIPS = ("zh", "x", "zl", "y")
VMEM_LIMIT = 48 * 1024 * 1024


def dot(a, b, dims):
    return lax.dot_general(a, b, (dims, ((), ())), preferred_element_type=F32)


def sigmoid(v):
    return 0.5 * jnp.tanh(0.5 * v) + 0.5


def columns(gains, scr):
    for n, ref in enumerate(gains):
        scr[2 * n : 2 * n + 2, :] = ref[...]
    return scr[...].T


def norm_channels(v, gain, bias):
    mean = jnp.mean(v, axis=0, keepdims=True)
    centered = v - mean
    var = jnp.mean(centered * centered, axis=0, keepdims=True)
    return centered * lax.rsqrt(var + 1e-05) * gain + bias


def swap_groups(v):
    lane = lax.broadcasted_iota(jnp.int32, v[0].shape, v[0].ndim - 1)
    low = lane < 64
    even = (lane // 32) % 2 == 0
    axis = v[0].ndim - 1

    def exchange(a, b, keep, up, down):
        return jnp.where(keep, a, pltpu.roll(b, up, axis)), jnp.where(keep, pltpu.roll(a, down, axis), b)

    a0, a2 = exchange(v[0], v[2], low, 64, 64)
    a1, a3 = exchange(v[1], v[3], low, 64, 64)
    b0, b1 = exchange(a0, a1, even, 32, 96)
    b2, b3 = exchange(a2, a3, even, 32, 96)
    return [b0, b1, b2, b3]


def first_mask(mask):
    m = mask[...].astype(F32)
    return jnp.concatenate([m[8 * q : 8 * q + 8] for q in range(4)], axis=1)


def transposed(w):
    return w.astype(F32).T.astype(BF16)


def transposed_halved(w):
    t = w.astype(F32).T
    hid = t.shape[0] // 4
    row = lax.broadcasted_iota(jnp.int32, t.shape, 0)
    return jnp.where((row // hid) % 2 == 0, 0.5 * t, t).astype(BF16)


def lanes_of(a):
    return slice(128 * a, 128 * a + 128)


def gated(proj, mask, scr):
    hid = proj.shape[0] // 4
    for a in range(8):
        lanes = lanes_of(a)
        row = 0.5 * mask[a : a + 1, :]
        left = row * proj[hid : 2 * hid, lanes] * (jnp.tanh(proj[:hid, lanes]) + 1.0)
        right = row * proj[3 * hid :, lanes] * (jnp.tanh(proj[2 * hid : 3 * hid, lanes]) + 1.0)
        scr[pl.ds(a, hid, stride=16), :] = left
        scr[pl.ds(a + 8, hid, stride=16), :] = right


def begin_kernel(*refs):
    inputs, (sent, pair_t, normed_t, mask_out, cols) = refs[:7], refs[7:12]
    local, (scr, gains, proj, sems) = refs[12:19], refs[19:]
    parts = [(inputs[0].at[8 * n : 8 * n + 8], local[0].at[8 * n : 8 * n + 8]) for n in range(4)]
    parts += [(inputs[2].at[0], local[2]), (inputs[1], local[1])] + list(zip(inputs[3:], local[3:]))
    copies = [pltpu.make_async_copy(src, dst, sems.at[n]) for n, (src, dst) in enumerate(parts)]
    for copy in copies:
        copy.start()
    for copy in copies:
        copy.wait()
    pair, mask, proj_w = local[:3]
    col = columns(local[3:], gains)
    cols[...] = col
    m8 = first_mask(mask)
    mask_out[...] = m8
    w_t = transposed_halved(proj_w[...])
    for a in range(8):
        block = jnp.concatenate([pair[8 * q + a] for q in range(4)], axis=0).astype(F32).T
        pair_t[:, lanes_of(a)] = block.astype(BF16)
        normed_t[:, lanes_of(a)] = norm_channels(block, col[:, 0:1], col[:, 2:3]).astype(BF16)
    proj[...] = dot(w_t, normed_t[...], ((1,), (0,)))
    gated(proj, m8, scr)
    sent[...] = scr[...].astype(BF16)


def statistics(got, tri):
    v = got[...].astype(F32)
    tri[...] = v
    v = v.reshape(8, 16, 8, 128)
    mean = jnp.mean(jnp.mean(v, axis=1), axis=0)
    centered = v - mean[None, None]
    return mean, lax.rsqrt(jnp.mean(jnp.mean(centered * centered, axis=1), axis=0) + 1e-05)


def norm_chunks(got, tri, gain, bias, out):
    mean, rstd = statistics(got, tri)
    chans = out.shape[0]
    for a in range(8):
        v = tri[pl.ds(a, chans, stride=8), :]
        out[:, lanes_of(a)] = ((v - mean[a : a + 1]) * rstd[a : a + 1] * gain + bias).astype(BF16)


def middle_kernel(got, pair_t, gate, mask, cols, w_t, out_t, sent, state_out, normed_out, tri, scr, proj, upd, tn):
    col = cols[...]
    norm_chunks(got, tri, col[:, 4:5], col[:, 6:7], tn)
    upd[...] = dot(out_t[...], tn[...], ((1,), (0,)))
    for a in range(8):
        lanes = lanes_of(a)
        state = (pair_t[:, lanes].astype(F32) + gate[:, lanes] * upd[:, lanes]).astype(BF16)
        state_out[:, lanes] = state
        normed_out[:, lanes] = norm_channels(state.astype(F32), col[:, 1:2], col[:, 3:4]).astype(BF16)
    proj[...] = dot(w_t[...], normed_out[...], ((1,), (0,)))
    gated(proj, mask[...], scr)
    sent[...] = scr[...].astype(BF16)


def end_kernel(got, state_t, gate, cols, out_t, out, tri, upd, tn):
    col = cols[...]
    norm_chunks(got, tri, col[:, 5:6], col[:, 7:8], tn)
    upd[...] = dot(out_t[...], tn[...], ((1,), (0,)))
    for a in range(8):
        lanes = lanes_of(a)
        state = (state_t[:, lanes].astype(F32) + gate[:, lanes] * upd[:, lanes]).T.astype(BF16)
        out[:, a] = state.reshape(4, 32, 128)


def gather_groups(v, out):
    v = v.astype(F32)
    for h in range(2):
        for q, t in enumerate(swap_groups([v[:, 4 * h + g] for g in range(4)])):
            out[:, q, :, 128 * h : 128 * h + 128] = t


def scatter_groups(prod, store):
    v = prod.reshape(-1, 4, 8, 256)
    for h in range(2):
        lanes = slice(128 * h, 128 * h + 128)
        for g, t in enumerate(swap_groups([v[:, q, :, lanes] for q in range(4)])):
            store(4 * h + g, t)


def outgoing_chunks(lm, rm, chunks):
    prod = dot(lm, rm, ((1,), (1,)))

    def store(c, t):
        chunks[:, c] = t

    scatter_groups(prod, store)
    return chunks[...].reshape(1024, 128)


def outgoing_right(got, parity, right):
    gather_groups(got[:, parity].astype(F32)[:, :, 8:], right)
    return right[...].reshape(256, 256).astype(BF16)


def outgoing_send_kernel(got, send, lm, left, right, chunks):
    gather_groups(got[...].astype(F32).reshape(16, 8, 16, 128)[:, :, :8], left)
    lm[...] = left[...].reshape(512, 256).astype(BF16)
    rm = outgoing_right(got, 1 - lax.axis_index("core"), right)
    send[...] = outgoing_chunks(lm[...], rm, chunks).astype(BF16)


def outgoing_keep_kernel(got, lm, normed_t, proj_w, gate_w, out_w, keep, gate, w_t, out_t, right, chunks):
    keep[...] = outgoing_chunks(lm[...], outgoing_right(got, lax.axis_index("core"), right), chunks)
    gate[...] = sigmoid(dot(transposed(gate_w[0]), normed_t[...], ((1,), (0,))))
    w_t[...] = transposed_halved(proj_w[1])
    out_t[...] = transposed(out_w[0])


def incoming_left_kernel(got, lm, left):
    gather_groups(got[...].astype(F32).reshape(16, 8, 16, 128)[:, :, :8], left)
    lm[...] = left[...].reshape(512, 256).astype(BF16)


def incoming_near_kernel(got, lm, normed_t, gate_w, out_w, near, rm, gate, out_t, right):
    gather_groups(got[...].astype(F32).reshape(16, 8, 16, 128)[:, :, 8:], right)
    rm[...] = right[...].reshape(512, 256).astype(BF16)

    def store(c, t):
        near[:, c] = t

    scatter_groups(dot(lm[...], rm[...], ((0,), (0,))), store)
    gate[...] = sigmoid(dot(transposed(gate_w[1]), normed_t[...], ((1,), (0,))))
    out_t[...] = transposed(out_w[1])


def incoming_far_kernel(far, rm, near, send, chunks):
    core = lax.axis_index("core")
    chunks[:, core] = near[...]

    def store(c, t):
        chunks[:, 1 - core, c] = t

    scatter_groups(dot(far[...], rm[...], ((0,), (0,))), store)
    send[...] = chunks[...].reshape(1024, 128).astype(BF16)


def call(kernel, outs, scratch, flops=0):
    return pl.pallas_call(
        kernel,
        out_shape=[jax.ShapeDtypeStruct(shape, dtype) for shape, dtype in outs],
        scratch_shapes=[pltpu.VMEM(shape, dtype) for shape, dtype in scratch],
        compiler_params=pltpu.CompilerParams(vmem_limit_bytes=VMEM_LIMIT),
        cost_estimate=pl.CostEstimate(flops=flops, bytes_accessed=1 << 20, transcendentals=1 << 17) if flops else None,
    )


def body(pair, mask, proj_w, gate_w, out_w, ig, ib, mg, mb):
    def exchange(v):
        return lax.all_to_all(v, CHIPS, 0, 0, tiled=True)

    def swap(v):
        return lax.ppermute(v, "core", [(0, 1), (1, 0)])

    first = (pair, mask, proj_w, ig, ib, mg, mb)
    sent, pair_t, normed_t, m8, cols = pl.pallas_call(
        begin_kernel,
        in_specs=[pl.BlockSpec(memory_space=pl.ANY)] * 7,
        out_shape=[
            jax.ShapeDtypeStruct((2048, 128), BF16),
            jax.ShapeDtypeStruct((128, 1024), BF16),
            jax.ShapeDtypeStruct((128, 1024), BF16),
            jax.ShapeDtypeStruct((8, 128), F32),
            jax.ShapeDtypeStruct((128, 8), F32),
        ],
        scratch_shapes=[pltpu.VMEM(v.shape[1:] if v is proj_w else v.shape, v.dtype) for v in first]
        + [
            pltpu.VMEM((2048, 128), F32),
            pltpu.VMEM((8, 128), F32),
            pltpu.VMEM((512, 1024), F32),
            pltpu.SemaphoreType.DMA((10,)),
        ],
        compiler_params=pltpu.CompilerParams(vmem_limit_bytes=VMEM_LIMIT),
    )(*(pltpu.with_memory_space_constraint(v, pltpu.HBM) for v in first))
    wide = (128, 1024)
    square = (16, 4, 8, 256)
    half = (8, 4, 8, 256)
    got = exchange(sent).reshape(8, 2, 8, 16, 128)
    send, lm = call(
        outgoing_send_kernel,
        [((1024, 128), BF16), ((512, 256), BF16)],
        [(square, F32), (half, F32), ((16, 8, 8, 128), F32)],
    )(got)
    far = swap(send)
    keep, gate, w_t, out_t = call(
        outgoing_keep_kernel,
        [((1024, 128), F32), (wide, F32), ((512, 128), BF16), ((128, 128), BF16)],
        [(half, F32), ((16, 8, 8, 128), F32)],
        1 << 28,
    )(got, lm, normed_t, proj_w, gate_w, out_w)
    got = exchange((keep + far.astype(F32)).astype(BF16))
    sent, state_t, normed_t = call(
        middle_kernel,
        [((2048, 128), BF16), (wide, BF16), (wide, BF16)],
        [((1024, 128), F32), ((2048, 128), F32), ((512, 1024), F32), (wide, F32), (wide, BF16)],
    )(got, pair_t, gate, m8, cols, w_t, out_t)
    got = exchange(sent).reshape(8, 2, 8, 16, 128)
    (lm,) = call(incoming_left_kernel, [((512, 256), BF16)], [(square, F32)])(got)
    far = swap(lm)
    near, rm, gate, out_t = call(
        incoming_near_kernel,
        [((8, 8, 8, 128), F32), ((512, 256), BF16), (wide, F32), ((128, 128), BF16)],
        [(square, F32)],
        1 << 28,
    )(got, lm, normed_t, gate_w, out_w)
    (send,) = call(incoming_far_kernel, [((1024, 128), BF16)], [((8, 2, 8, 8, 128), F32)])(far, rm, near)
    (out,) = call(
        end_kernel,
        [((4, 8, 32, 128), BF16)],
        [((1024, 128), F32), (wide, F32), (wide, BF16)],
    )(exchange(send), state_t, gate, cols, out_t)
    return out.reshape(32, 32, 128)


def solution(mesh):
    fine = Mesh(mesh.devices.reshape(4, 4, 2, 4, 2), ("zh", "x", "zl", "y", "core"))
    block = P(("zh", "x"), ("zl", "y", "core"))
    return jax.shard_map(
        body,
        mesh=fine,
        in_specs=(block, block, P(), P(), P(), P(), P(), P(), P()),
        out_specs=block,
        check_vma=False,
    )
```

```python
import jax
import jax.numpy as jnp
from jax import lax
from jax.experimental import pallas as pl
from jax.experimental.pallas import tpu as pltpu
from jax.sharding import Mesh
from jax.sharding import PartitionSpec as P

F32 = jnp.float32
BF16 = jnp.bfloat16
CHIPS = ("zh", "x", "zl", "y")
VMEM_LIMIT = 48 * 1024 * 1024
SCR = (2048 + 16, 128)
TRI = (1024 + 8, 128)


def dot(a, b, dims):
    return lax.dot_general(a, b, (dims, ((), ())), preferred_element_type=F32)


def sigmoid(v):
    return 0.5 * jnp.tanh(0.5 * v) + 0.5


def columns(gains, scr):
    for n, ref in enumerate(gains):
        scr[2 * n : 2 * n + 2, :] = ref[...]
    return scr[...].T


def norm_channels(v, gain, bias):
    mean = jnp.mean(v, axis=0, keepdims=True)
    centered = v - mean
    var = jnp.mean(centered * centered, axis=0, keepdims=True)
    return centered * lax.rsqrt(var + 1e-05) * gain + bias


def swap_groups(v):
    lane = lax.broadcasted_iota(jnp.int32, v[0].shape, v[0].ndim - 1)
    low = lane < 64
    even = (lane // 32) % 2 == 0
    axis = v[0].ndim - 1

    def exchange(a, b, keep, up, down):
        return jnp.where(keep, a, pltpu.roll(b, up, axis)), jnp.where(keep, pltpu.roll(a, down, axis), b)

    a0, a2 = exchange(v[0], v[2], low, 64, 64)
    a1, a3 = exchange(v[1], v[3], low, 64, 64)
    b0, b1 = exchange(a0, a1, even, 32, 96)
    b2, b3 = exchange(a2, a3, even, 32, 96)
    return [b0, b1, b2, b3]


def first_mask(mask):
    m = mask[...].astype(F32)
    return jnp.concatenate([m[8 * q : 8 * q + 8] for q in range(4)], axis=1)


def transposed(w):
    return w.astype(F32).T.astype(BF16)


def transposed_halved(w):
    t = w.astype(F32).T
    hid = t.shape[0] // 4
    row = lax.broadcasted_iota(jnp.int32, t.shape, 0)
    return jnp.where((row // hid) % 2 == 0, 0.5 * t, t).astype(BF16)


def lanes_of(a):
    return slice(128 * a, 128 * a + 128)


def gated(proj, mask, scr):
    hid = proj.shape[0] // 4
    for a in range(8):
        lanes = lanes_of(a)
        row = 0.5 * mask[a : a + 1, :]
        left = row * proj[hid : 2 * hid, lanes] * (jnp.tanh(proj[:hid, lanes]) + 1.0)
        right = row * proj[3 * hid :, lanes] * (jnp.tanh(proj[2 * hid : 3 * hid, lanes]) + 1.0)
        scr[pl.ds(a, hid, stride=16), :] = left
        scr[pl.ds(a + 8, hid, stride=16), :] = right


def begin_kernel(*refs):
    inputs, (sent, pair_t, normed_t, mask_out, cols) = refs[:7], refs[7:12]
    local, (scr, gains, proj, sems) = refs[12:19], refs[19:]
    parts = [(inputs[0].at[8 * n : 8 * n + 8], local[0].at[8 * n : 8 * n + 8]) for n in range(4)]
    parts += [(inputs[2].at[0], local[2]), (inputs[1], local[1])] + list(zip(inputs[3:], local[3:]))
    copies = [pltpu.make_async_copy(src, dst, sems.at[n]) for n, (src, dst) in enumerate(parts)]
    for copy in copies:
        copy.start()
    for copy in copies:
        copy.wait()
    pair, mask, proj_w = local[:3]
    col = columns(local[3:], gains)
    cols[...] = col
    m8 = first_mask(mask)
    mask_out[...] = m8
    w_t = transposed_halved(proj_w[...])
    for a in range(8):
        block = jnp.concatenate([pair[8 * q + a] for q in range(4)], axis=0).astype(F32).T
        pair_t[:, lanes_of(a)] = block.astype(BF16)
        normed_t[:, lanes_of(a)] = norm_channels(block, col[:, 0:1], col[:, 2:3]).astype(BF16)
    proj[...] = dot(w_t, normed_t[...], ((1,), (0,)))
    gated(proj, m8, scr)
    sent[...] = scr[0:2048, :].astype(BF16)


def statistics(got, tri):
    v = got[...].astype(F32)
    tri[0:1024, :] = v
    v = v.reshape(8, 16, 8, 128)
    mean = jnp.mean(jnp.mean(v, axis=1), axis=0)
    centered = v - mean[None, None]
    return mean, lax.rsqrt(jnp.mean(jnp.mean(centered * centered, axis=1), axis=0) + 1e-05)


def norm_chunks(got, tri, gain, bias, out):
    mean, rstd = statistics(got, tri)
    chans = out.shape[0]
    for a in range(8):
        v = tri[pl.ds(a, chans, stride=8), :]
        out[:, lanes_of(a)] = ((v - mean[a : a + 1]) * rstd[a : a + 1] * gain + bias).astype(BF16)


def middle_kernel(got, pair_t, gate, mask, cols, w_t, out_t, sent, state_out, normed_out, tri, scr, proj, upd, tn):
    col = cols[...]
    norm_chunks(got, tri, col[:, 4:5], col[:, 6:7], tn)
    upd[...] = dot(out_t[...], tn[...], ((1,), (0,)))
    for a in range(8):
        lanes = lanes_of(a)
        state = (pair_t[:, lanes].astype(F32) + gate[:, lanes] * upd[:, lanes]).astype(BF16)
        state_out[:, lanes] = state
        normed_out[:, lanes] = norm_channels(state.astype(F32), col[:, 1:2], col[:, 3:4]).astype(BF16)
    proj[...] = dot(w_t[...], normed_out[...], ((1,), (0,)))
    gated(proj, mask[...], scr)
    sent[...] = scr[0:2048, :].astype(BF16)


def end_kernel(got, state_t, gate, cols, out_t, out, tri, upd, tn):
    col = cols[...]
    norm_chunks(got, tri, col[:, 5:6], col[:, 7:8], tn)
    upd[...] = dot(out_t[...], tn[...], ((1,), (0,)))
    for a in range(8):
        lanes = lanes_of(a)
        state = (state_t[:, lanes].astype(F32) + gate[:, lanes] * upd[:, lanes]).T.astype(BF16)
        out[:, a] = state.reshape(4, 32, 128)


def gather_groups(v, out):
    v = v.astype(F32)
    for h in range(2):
        for q, t in enumerate(swap_groups([v[:, 4 * h + g] for g in range(4)])):
            out[:, q, :, 128 * h : 128 * h + 128] = t


def scatter_groups(prod, store):
    v = prod.reshape(-1, 4, 8, 256)
    for h in range(2):
        lanes = slice(128 * h, 128 * h + 128)
        for g, t in enumerate(swap_groups([v[:, q, :, lanes] for q in range(4)])):
            store(4 * h + g, t)


def outgoing_chunks(lm, rm, chunks):
    prod = dot(lm, rm, ((1,), (1,)))

    def store(c, t):
        chunks[:, c] = t

    scatter_groups(prod, store)
    return chunks[...].reshape(1024, 128)


def outgoing_right(got, parity, right):
    gather_groups(got[:, parity].astype(F32)[:, :, 8:], right)
    return right[...].reshape(256, 256).astype(BF16)


def outgoing_send_kernel(got, send, lm, left, right, chunks):
    gather_groups(got[...].astype(F32).reshape(16, 8, 16, 128)[:, :, :8], left)
    lm[...] = left[...].reshape(512, 256).astype(BF16)
    rm = outgoing_right(got, 1 - lax.axis_index("core"), right)
    send[...] = outgoing_chunks(lm[...], rm, chunks).astype(BF16)


def outgoing_keep_kernel(got, lm, normed_t, proj_w, gate_w, out_w, keep, gate, w_t, out_t, right, chunks):
    keep[...] = outgoing_chunks(lm[...], outgoing_right(got, lax.axis_index("core"), right), chunks)
    gate[...] = sigmoid(dot(transposed(gate_w[0]), normed_t[...], ((1,), (0,))))
    w_t[...] = transposed_halved(proj_w[1])
    out_t[...] = transposed(out_w[0])


def incoming_left_kernel(got, lm, left):
    gather_groups(got[...].astype(F32).reshape(16, 8, 16, 128)[:, :, :8], left)
    lm[...] = left[...].reshape(512, 256).astype(BF16)


def incoming_near_kernel(got, lm, normed_t, gate_w, out_w, near, rm, gate, out_t, right):
    gather_groups(got[...].astype(F32).reshape(16, 8, 16, 128)[:, :, 8:], right)
    rm[...] = right[...].reshape(512, 256).astype(BF16)

    def store(c, t):
        near[:, c] = t

    scatter_groups(dot(lm[...], rm[...], ((0,), (0,))), store)
    gate[...] = sigmoid(dot(transposed(gate_w[1]), normed_t[...], ((1,), (0,))))
    out_t[...] = transposed(out_w[1])


def incoming_far_kernel(far, rm, near, send, chunks):
    core = lax.axis_index("core")
    chunks[:, core] = near[...]

    def store(c, t):
        chunks[:, 1 - core, c] = t

    scatter_groups(dot(far[...], rm[...], ((0,), (0,))), store)
    send[...] = chunks[...].reshape(1024, 128).astype(BF16)


def call(kernel, outs, scratch, flops=0):
    return pl.pallas_call(
        kernel,
        out_shape=[jax.ShapeDtypeStruct(shape, dtype) for shape, dtype in outs],
        scratch_shapes=[pltpu.VMEM(shape, dtype) for shape, dtype in scratch],
        compiler_params=pltpu.CompilerParams(vmem_limit_bytes=VMEM_LIMIT),
        cost_estimate=pl.CostEstimate(flops=flops, bytes_accessed=1 << 20, transcendentals=1 << 17) if flops else None,
    )


def body(pair, mask, proj_w, gate_w, out_w, ig, ib, mg, mb):
    def exchange(v):
        return lax.all_to_all(v, CHIPS, 0, 0, tiled=True)

    def swap(v):
        return lax.ppermute(v, "core", [(0, 1), (1, 0)])

    first = (pair, mask, proj_w, ig, ib, mg, mb)
    sent, pair_t, normed_t, m8, cols = pl.pallas_call(
        begin_kernel,
        in_specs=[pl.BlockSpec(memory_space=pl.ANY)] * 7,
        out_shape=[
            jax.ShapeDtypeStruct((2048, 128), BF16),
            jax.ShapeDtypeStruct((128, 1024), BF16),
            jax.ShapeDtypeStruct((128, 1024), BF16),
            jax.ShapeDtypeStruct((8, 128), F32),
            jax.ShapeDtypeStruct((128, 8), F32),
        ],
        scratch_shapes=[pltpu.VMEM(v.shape[1:] if v is proj_w else v.shape, v.dtype) for v in first]
        + [
            pltpu.VMEM(SCR, F32),
            pltpu.VMEM((8, 128), F32),
            pltpu.VMEM((512, 1024), F32),
            pltpu.SemaphoreType.DMA((10,)),
        ],
        compiler_params=pltpu.CompilerParams(vmem_limit_bytes=VMEM_LIMIT),
    )(*(pltpu.with_memory_space_constraint(v, pltpu.HBM) for v in first))
    wide = (128, 1024)
    square = (16, 4, 8, 256)
    half = (8, 4, 8, 256)
    got = exchange(sent).reshape(8, 2, 8, 16, 128)
    send, lm = call(
        outgoing_send_kernel,
        [((1024, 128), BF16), ((512, 256), BF16)],
        [(square, F32), (half, F32), ((16, 8, 8, 128), F32)],
    )(got)
    far = swap(send)
    keep, gate, w_t, out_t = call(
        outgoing_keep_kernel,
        [((1024, 128), F32), (wide, F32), ((512, 128), BF16), ((128, 128), BF16)],
        [(half, F32), ((16, 8, 8, 128), F32)],
        1 << 28,
    )(got, lm, normed_t, proj_w, gate_w, out_w)
    got = exchange((keep + far.astype(F32)).astype(BF16))
    sent, state_t, normed_t = call(
        middle_kernel,
        [((2048, 128), BF16), (wide, BF16), (wide, BF16)],
        [(TRI, F32), (SCR, F32), ((512, 1024), F32), (wide, F32), (wide, BF16)],
    )(got, pair_t, gate, m8, cols, w_t, out_t)
    got = exchange(sent).reshape(8, 2, 8, 16, 128)
    (lm,) = call(incoming_left_kernel, [((512, 256), BF16)], [(square, F32)])(got)
    far = swap(lm)
    near, rm, gate, out_t = call(
        incoming_near_kernel,
        [((8, 8, 8, 128), F32), ((512, 256), BF16), (wide, F32), ((128, 128), BF16)],
        [(square, F32)],
        1 << 28,
    )(got, lm, normed_t, gate_w, out_w)
    (send,) = call(incoming_far_kernel, [((1024, 128), BF16)], [((8, 2, 8, 8, 128), F32)])(far, rm, near)
    (out,) = call(
        end_kernel,
        [((4, 8, 32, 128), BF16)],
        [(TRI, F32), (wide, F32), (wide, BF16)],
    )(exchange(send), state_t, gate, cols, out_t)
    return out.reshape(32, 32, 128)


def solution(mesh):
    fine = Mesh(mesh.devices.reshape(4, 4, 2, 4, 2), ("zh", "x", "zl", "y", "core"))
    block = P(("zh", "x"), ("zl", "y", "core"))
    return jax.shard_map(
        body,
        mesh=fine,
        in_specs=(block, block, P(), P(), P(), P(), P(), P(), P()),
        out_specs=block,
        check_vma=False,
    )
```

```python
import jax
import jax.numpy as jnp
from jax import lax
from jax.experimental import pallas as pl
from jax.experimental.pallas import tpu as pltpu
from jax.sharding import Mesh
from jax.sharding import PartitionSpec as P

F32 = jnp.float32
BF16 = jnp.bfloat16
CHIPS = ("zh", "x", "zl", "y")
VMEM_LIMIT = 48 * 1024 * 1024
SCR = (2048 + 16, 128)
TRI = (1024 + 8, 128)


def dot(a, b, dims):
    return lax.dot_general(a, b, (dims, ((), ())), preferred_element_type=F32)


def sigmoid(v):
    return 0.5 * jnp.tanh(0.5 * v) + 0.5


def columns(gains, scr):
    for n, ref in enumerate(gains):
        scr[2 * n : 2 * n + 2, :] = ref[...]
    return scr[...].T


def norm_channels(v, gain, bias):
    mean = jnp.mean(v, axis=0, keepdims=True)
    centered = v - mean
    var = jnp.mean(centered * centered, axis=0, keepdims=True)
    return centered * lax.rsqrt(var + 1e-05) * gain + bias


def swap_groups(v):
    lane = lax.broadcasted_iota(jnp.int32, v[0].shape, v[0].ndim - 1)
    low = lane < 64
    even = (lane // 32) % 2 == 0
    axis = v[0].ndim - 1

    def exchange(a, b, keep, up, down):
        return jnp.where(keep, a, pltpu.roll(b, up, axis)), jnp.where(keep, pltpu.roll(a, down, axis), b)

    a0, a2 = exchange(v[0], v[2], low, 64, 64)
    a1, a3 = exchange(v[1], v[3], low, 64, 64)
    b0, b1 = exchange(a0, a1, even, 32, 96)
    b2, b3 = exchange(a2, a3, even, 32, 96)
    return [b0, b1, b2, b3]


def first_mask(mask):
    m = mask[...].astype(F32)
    return jnp.concatenate([m[8 * q : 8 * q + 8] for q in range(4)], axis=1)


def transposed(w):
    return w.astype(F32).T.astype(BF16)


def transposed_halved(w):
    t = w.astype(F32).T
    hid = t.shape[0] // 4
    row = lax.broadcasted_iota(jnp.int32, t.shape, 0)
    return jnp.where((row // hid) % 2 == 0, 0.5 * t, t).astype(BF16)


def lanes_of(a):
    return slice(128 * a, 128 * a + 128)


def gated(proj, mask, scr):
    hid = proj.shape[0] // 4
    for a in range(8):
        lanes = lanes_of(a)
        row = 0.5 * mask[a : a + 1, :]
        left = row * proj[hid : 2 * hid, lanes] * (jnp.tanh(proj[:hid, lanes]) + 1.0)
        right = row * proj[3 * hid :, lanes] * (jnp.tanh(proj[2 * hid : 3 * hid, lanes]) + 1.0)
        scr[pl.ds(a, hid, stride=16), :] = left
        scr[pl.ds(a + 8, hid, stride=16), :] = right


def begin_kernel(*refs):
    inputs, (sent, pair_t, normed_t, mask_out, cols) = refs[:7], refs[7:12]
    local, (scr, gains, proj, sems) = refs[12:19], refs[19:]
    parts = [(inputs[0].at[8 * n : 8 * n + 8], local[0].at[8 * n : 8 * n + 8]) for n in range(4)]
    parts += [(inputs[2].at[0], local[2]), (inputs[1], local[1])] + list(zip(inputs[3:], local[3:]))
    copies = [pltpu.make_async_copy(src, dst, sems.at[n]) for n, (src, dst) in enumerate(parts)]
    for copy in copies:
        copy.start()
    for copy in copies:
        copy.wait()
    pair, mask, proj_w = local[:3]
    col = columns(local[3:], gains)
    cols[...] = col
    m8 = first_mask(mask)
    mask_out[...] = m8
    w_t = transposed_halved(proj_w[...])
    for a in range(8):
        block = jnp.concatenate([pair[8 * q + a] for q in range(4)], axis=0).astype(F32).T
        pair_t[:, lanes_of(a)] = block.astype(BF16)
        normed_t[:, lanes_of(a)] = norm_channels(block, col[:, 0:1], col[:, 2:3]).astype(BF16)
    proj[...] = dot(w_t, normed_t[...], ((1,), (0,)))
    gated(proj, m8, scr)
    sent[...] = scr[0:2048, :].astype(BF16)


def statistics(got, tri):
    v = got[...].astype(F32)
    tri[0:1024, :] = v
    v = v.reshape(8, 16, 8, 128)
    mean = jnp.mean(jnp.mean(v, axis=1), axis=0)
    centered = v - mean[None, None]
    return mean, lax.rsqrt(jnp.mean(jnp.mean(centered * centered, axis=1), axis=0) + 1e-05)


def norm_chunks(got, tri, gain, bias, out):
    mean, rstd = statistics(got, tri)
    chans = out.shape[0]
    for a in range(8):
        v = tri[pl.ds(a, chans, stride=8), :]
        out[:, lanes_of(a)] = ((v - mean[a : a + 1]) * rstd[a : a + 1] * gain + bias).astype(BF16)


def middle_kernel(got, pair_t, gate, mask, cols, w_t, out_t, sent, state_out, normed_out, tri, scr, proj, upd, tn):
    col = cols[...]
    norm_chunks(got, tri, col[:, 4:5], col[:, 6:7], tn)
    upd[...] = dot(out_t[...], tn[...], ((1,), (0,)))
    for a in range(8):
        lanes = lanes_of(a)
        state = (pair_t[:, lanes].astype(F32) + gate[:, lanes] * upd[:, lanes]).astype(BF16)
        state_out[:, lanes] = state
        normed_out[:, lanes] = norm_channels(state.astype(F32), col[:, 1:2], col[:, 3:4]).astype(BF16)
    proj[...] = dot(w_t[...], normed_out[...], ((1,), (0,)))
    gated(proj, mask[...], scr)
    sent[...] = scr[0:2048, :].astype(BF16)


def end_kernel(got, state_t, gate, cols, out_t, out, tri, upd, tn):
    col = cols[...]
    norm_chunks(got, tri, col[:, 5:6], col[:, 7:8], tn)
    upd[...] = dot(out_t[...], tn[...], ((1,), (0,)))
    for a in range(8):
        lanes = lanes_of(a)
        state = (state_t[:, lanes].astype(F32) + gate[:, lanes] * upd[:, lanes]).T.astype(BF16)
        out[:, a] = state.reshape(4, 32, 128)


def gather_groups(v, out):
    v = v.astype(F32)
    for h in range(2):
        for q, t in enumerate(swap_groups([v[:, 4 * h + g] for g in range(4)])):
            out[:, q, :, 128 * h : 128 * h + 128] = t


def scatter_groups(prod, store):
    v = prod.reshape(-1, 4, 8, 256)
    for h in range(2):
        lanes = slice(128 * h, 128 * h + 128)
        for g, t in enumerate(swap_groups([v[:, q, :, lanes] for q in range(4)])):
            store(4 * h + g, t)


def outgoing_chunks(lm, rm, chunks):
    prod = dot(lm, rm, ((1,), (1,)))

    def store(c, t):
        chunks[:, c] = t

    scatter_groups(prod, store)
    return chunks[...].reshape(1024, 128)


def outgoing_right(got, parity, right):
    gather_groups(got[:, parity].astype(F32)[:, :, 8:], right)
    return right[...].reshape(256, 256).astype(BF16)


def outgoing_send_kernel(got, send, lm, left, right, chunks):
    gather_groups(got[...].astype(F32).reshape(16, 8, 16, 128)[:, :, :8], left)
    lm[...] = left[...].reshape(512, 256).astype(BF16)
    rm = outgoing_right(got, 1 - lax.axis_index("core"), right)
    send[...] = outgoing_chunks(lm[...], rm, chunks).astype(BF16)


def outgoing_own(got, lm, right, chunks):
    return outgoing_chunks(lm[...], outgoing_right(got, lax.axis_index("core"), right), chunks)


def outgoing_keep_kernel(got, lm, normed_t, proj_w, gate_w, out_w, keep, gate, w_t, out_t, right, chunks):
    gate[...] = sigmoid(dot(transposed(gate_w[0]), normed_t[...], ((1,), (0,))))
    w_t[...] = transposed_halved(proj_w[1])
    out_t[...] = transposed(out_w[0])

    @pl.when(lax.axis_index("core") == 1)
    def _():
        keep[...] = outgoing_own(got, lm, right, chunks)


def outgoing_sum_kernel(got, lm, keep, far, total, right, chunks):
    core = lax.axis_index("core")

    @pl.when(core == 0)
    def _():
        total[...] = (outgoing_own(got, lm, right, chunks) + far[...].astype(F32)).astype(BF16)

    @pl.when(core == 1)
    def _():
        total[...] = (keep[...] + far[...].astype(F32)).astype(BF16)


def incoming_left_kernel(got, lm, left):
    gather_groups(got[...].astype(F32).reshape(16, 8, 16, 128)[:, :, :8], left)
    lm[...] = left[...].reshape(512, 256).astype(BF16)


def incoming_near_kernel(got, lm, normed_t, gate_w, out_w, near, rm, gate, out_t, right):
    gather_groups(got[...].astype(F32).reshape(16, 8, 16, 128)[:, :, 8:], right)
    rm[...] = right[...].reshape(512, 256).astype(BF16)

    def store(c, t):
        near[:, c] = t

    scatter_groups(dot(lm[...], rm[...], ((0,), (0,))), store)
    gate[...] = sigmoid(dot(transposed(gate_w[1]), normed_t[...], ((1,), (0,))))
    out_t[...] = transposed(out_w[1])


def incoming_far_kernel(far, rm, near, send, chunks):
    core = lax.axis_index("core")
    chunks[:, core] = near[...]

    def store(c, t):
        chunks[:, 1 - core, c] = t

    scatter_groups(dot(far[...], rm[...], ((0,), (0,))), store)
    send[...] = chunks[...].reshape(1024, 128).astype(BF16)


def call(kernel, outs, scratch, flops=0):
    return pl.pallas_call(
        kernel,
        out_shape=[jax.ShapeDtypeStruct(shape, dtype) for shape, dtype in outs],
        scratch_shapes=[pltpu.VMEM(shape, dtype) for shape, dtype in scratch],
        compiler_params=pltpu.CompilerParams(vmem_limit_bytes=VMEM_LIMIT),
        cost_estimate=pl.CostEstimate(flops=flops, bytes_accessed=1 << 20, transcendentals=1 << 17) if flops else None,
    )


def body(pair, mask, proj_w, gate_w, out_w, ig, ib, mg, mb):
    def exchange(v):
        return lax.all_to_all(v, CHIPS, 0, 0, tiled=True)

    def swap(v):
        return lax.ppermute(v, "core", [(0, 1), (1, 0)])

    first = (pair, mask, proj_w, ig, ib, mg, mb)
    sent, pair_t, normed_t, m8, cols = pl.pallas_call(
        begin_kernel,
        in_specs=[pl.BlockSpec(memory_space=pl.ANY)] * 7,
        out_shape=[
            jax.ShapeDtypeStruct((2048, 128), BF16),
            jax.ShapeDtypeStruct((128, 1024), BF16),
            jax.ShapeDtypeStruct((128, 1024), BF16),
            jax.ShapeDtypeStruct((8, 128), F32),
            jax.ShapeDtypeStruct((128, 8), F32),
        ],
        scratch_shapes=[pltpu.VMEM(v.shape[1:] if v is proj_w else v.shape, v.dtype) for v in first]
        + [
            pltpu.VMEM(SCR, F32),
            pltpu.VMEM((8, 128), F32),
            pltpu.VMEM((512, 1024), F32),
            pltpu.SemaphoreType.DMA((10,)),
        ],
        compiler_params=pltpu.CompilerParams(vmem_limit_bytes=VMEM_LIMIT),
    )(*(pltpu.with_memory_space_constraint(v, pltpu.HBM) for v in first))
    wide = (128, 1024)
    square = (16, 4, 8, 256)
    half = (8, 4, 8, 256)
    got = exchange(sent).reshape(8, 2, 8, 16, 128)
    send, lm = call(
        outgoing_send_kernel,
        [((1024, 128), BF16), ((512, 256), BF16)],
        [(square, F32), (half, F32), ((16, 8, 8, 128), F32)],
    )(got)
    far = swap(send)
    keep, gate, w_t, out_t = call(
        outgoing_keep_kernel,
        [((1024, 128), F32), (wide, F32), ((512, 128), BF16), ((128, 128), BF16)],
        [(half, F32), ((16, 8, 8, 128), F32)],
        1 << 28,
    )(got, lm, normed_t, proj_w, gate_w, out_w)
    (total,) = call(
        outgoing_sum_kernel,
        [((1024, 128), BF16)],
        [(half, F32), ((16, 8, 8, 128), F32)],
    )(got, lm, keep, far)
    got = exchange(total)
    sent, state_t, normed_t = call(
        middle_kernel,
        [((2048, 128), BF16), (wide, BF16), (wide, BF16)],
        [(TRI, F32), (SCR, F32), ((512, 1024), F32), (wide, F32), (wide, BF16)],
    )(got, pair_t, gate, m8, cols, w_t, out_t)
    got = exchange(sent).reshape(8, 2, 8, 16, 128)
    (lm,) = call(incoming_left_kernel, [((512, 256), BF16)], [(square, F32)])(got)
    far = swap(lm)
    near, rm, gate, out_t = call(
        incoming_near_kernel,
        [((8, 8, 8, 128), F32), ((512, 256), BF16), (wide, F32), ((128, 128), BF16)],
        [(square, F32)],
        1 << 28,
    )(got, lm, normed_t, gate_w, out_w)
    (send,) = call(incoming_far_kernel, [((1024, 128), BF16)], [((8, 2, 8, 8, 128), F32)])(far, rm, near)
    (out,) = call(
        end_kernel,
        [((4, 8, 32, 128), BF16)],
        [(TRI, F32), (wide, F32), (wide, BF16)],
    )(exchange(send), state_t, gate, cols, out_t)
    return out.reshape(32, 32, 128)


def solution(mesh):
    fine = Mesh(mesh.devices.reshape(4, 4, 2, 4, 2), ("zh", "x", "zl", "y", "core"))
    block = P(("zh", "x"), ("zl", "y", "core"))
    return jax.shard_map(
        body,
        mesh=fine,
        in_specs=(block, block, P(), P(), P(), P(), P(), P(), P()),
        out_specs=block,
        check_vma=False,
    )
```

```python
import jax
import jax.numpy as jnp
from jax import lax
from jax.experimental import pallas as pl
from jax.experimental.pallas import tpu as pltpu
from jax.sharding import Mesh
from jax.sharding import PartitionSpec as P

F32 = jnp.float32
BF16 = jnp.bfloat16
CHIPS = ("zh", "x", "zl", "y")
VMEM_LIMIT = 48 * 1024 * 1024
SCR = (2048 + 16, 128)
TRI = (1024 + 8, 128)


def dot(a, b, dims):
    return lax.dot_general(a, b, (dims, ((), ())), preferred_element_type=F32)


def sigmoid(v):
    return 0.5 * jnp.tanh(0.5 * v) + 0.5


def columns(gains, scr):
    for n, ref in enumerate(gains):
        scr[2 * n : 2 * n + 2, :] = ref[...]
    return scr[...].T


def norm_channels(v, gain, bias):
    mean = jnp.mean(v, axis=0, keepdims=True)
    centered = v - mean
    var = jnp.mean(centered * centered, axis=0, keepdims=True)
    return centered * lax.rsqrt(var + 1e-05) * gain + bias


def swap_groups(v):
    lane = lax.broadcasted_iota(jnp.int32, v[0].shape, v[0].ndim - 1)
    low = lane < 64
    even = (lane // 32) % 2 == 0
    axis = v[0].ndim - 1

    def exchange(a, b, keep, up, down):
        return jnp.where(keep, a, pltpu.roll(b, up, axis)), jnp.where(keep, pltpu.roll(a, down, axis), b)

    a0, a2 = exchange(v[0], v[2], low, 64, 64)
    a1, a3 = exchange(v[1], v[3], low, 64, 64)
    b0, b1 = exchange(a0, a1, even, 32, 96)
    b2, b3 = exchange(a2, a3, even, 32, 96)
    return [b0, b1, b2, b3]


def first_mask(mask):
    m = mask[...].astype(F32)
    return jnp.concatenate([m[8 * q : 8 * q + 8] for q in range(4)], axis=1)


def transposed(w):
    return w.astype(F32).T.astype(BF16)


def transposed_halved(w):
    t = w.astype(F32).T
    hid = t.shape[0] // 4
    row = lax.broadcasted_iota(jnp.int32, t.shape, 0)
    return jnp.where((row // hid) % 2 == 0, 0.5 * t, t).astype(BF16)


def lanes_of(a):
    return slice(128 * a, 128 * a + 128)


def gated(proj, mask, scr):
    hid = proj.shape[0] // 4
    for a in range(8):
        lanes = lanes_of(a)
        row = 0.5 * mask[a : a + 1, :]
        left = row * proj[hid : 2 * hid, lanes] * (jnp.tanh(proj[:hid, lanes]) + 1.0)
        right = row * proj[3 * hid :, lanes] * (jnp.tanh(proj[2 * hid : 3 * hid, lanes]) + 1.0)
        scr[pl.ds(a, hid, stride=16), :] = left
        scr[pl.ds(a + 8, hid, stride=16), :] = right


def begin_kernel(*refs):
    inputs, (sent, pair_t, normed_t, mask_out, cols) = refs[:7], refs[7:12]
    local, (scr, gains, proj, sems) = refs[12:19], refs[19:]
    early = [(inputs[0].at[8 * n : 8 * n + 8], local[0].at[8 * n : 8 * n + 8]) for n in range(4)]
    early += list(zip(inputs[3:], local[3:]))
    late = [(inputs[2].at[0], local[2]), (inputs[1], local[1])]
    copies = [pltpu.make_async_copy(src, dst, sems.at[n]) for n, (src, dst) in enumerate(early + late)]
    for copy in copies:
        copy.start()
    for copy in copies[: len(early)]:
        copy.wait()
    pair, mask, proj_w = local[:3]
    col = columns(local[3:], gains)
    cols[...] = col
    for a in range(8):
        block = jnp.concatenate([pair[8 * q + a] for q in range(4)], axis=0).astype(F32).T
        pair_t[:, lanes_of(a)] = block.astype(BF16)
        normed_t[:, lanes_of(a)] = norm_channels(block, col[:, 0:1], col[:, 2:3]).astype(BF16)
    for copy in copies[len(early) :]:
        copy.wait()
    m8 = first_mask(mask)
    mask_out[...] = m8
    w_t = transposed_halved(proj_w[...])
    proj[...] = dot(w_t, normed_t[...], ((1,), (0,)))
    gated(proj, m8, scr)
    sent[...] = scr[0:2048, :].astype(BF16)


def statistics(got, tri):
    v = got[...].astype(F32)
    tri[0:1024, :] = v
    v = v.reshape(8, 16, 8, 128)
    mean = jnp.mean(jnp.mean(v, axis=1), axis=0)
    centered = v - mean[None, None]
    return mean, lax.rsqrt(jnp.mean(jnp.mean(centered * centered, axis=1), axis=0) + 1e-05)


def norm_chunks(got, tri, gain, bias, out):
    mean, rstd = statistics(got, tri)
    chans = out.shape[0]
    for a in range(8):
        v = tri[pl.ds(a, chans, stride=8), :]
        out[:, lanes_of(a)] = ((v - mean[a : a + 1]) * rstd[a : a + 1] * gain + bias).astype(BF16)


def middle_kernel(got, pair_t, gate, mask, cols, w_t, out_t, sent, state_out, normed_out, tri, scr, proj, upd, tn):
    col = cols[...]
    norm_chunks(got, tri, col[:, 4:5], col[:, 6:7], tn)
    upd[...] = dot(out_t[...], tn[...], ((1,), (0,)))
    for a in range(8):
        lanes = lanes_of(a)
        state = (pair_t[:, lanes].astype(F32) + gate[:, lanes] * upd[:, lanes]).astype(BF16)
        state_out[:, lanes] = state
        normed_out[:, lanes] = norm_channels(state.astype(F32), col[:, 1:2], col[:, 3:4]).astype(BF16)
    proj[...] = dot(w_t[...], normed_out[...], ((1,), (0,)))
    gated(proj, mask[...], scr)
    sent[...] = scr[0:2048, :].astype(BF16)


def end_kernel(got, state_t, gate, cols, out_t, out, tri, upd, tn):
    col = cols[...]
    norm_chunks(got, tri, col[:, 5:6], col[:, 7:8], tn)
    upd[...] = dot(out_t[...], tn[...], ((1,), (0,)))
    for a in range(8):
        lanes = lanes_of(a)
        state = (state_t[:, lanes].astype(F32) + gate[:, lanes] * upd[:, lanes]).T.astype(BF16)
        out[:, a] = state.reshape(4, 32, 128)


def gather_groups(v, out):
    v = v.astype(F32)
    for h in range(2):
        for q, t in enumerate(swap_groups([v[:, 4 * h + g] for g in range(4)])):
            out[:, q, :, 128 * h : 128 * h + 128] = t


def scatter_groups(prod, store):
    v = prod.reshape(-1, 4, 8, 256)
    for h in range(2):
        lanes = slice(128 * h, 128 * h + 128)
        for g, t in enumerate(swap_groups([v[:, q, :, lanes] for q in range(4)])):
            store(4 * h + g, t)


def outgoing_chunks(lm, rm, chunks):
    prod = dot(lm, rm, ((1,), (1,)))

    def store(c, t):
        chunks[:, c] = t

    scatter_groups(prod, store)
    return chunks[...].reshape(1024, 128)


def outgoing_right(got, parity, right):
    gather_groups(got[:, parity].astype(F32)[:, :, 8:], right)
    return right[...].reshape(256, 256).astype(BF16)


def outgoing_send_kernel(got, send, lm, left, right, chunks):
    gather_groups(got[...].astype(F32).reshape(16, 8, 16, 128)[:, :, :8], left)
    lm[...] = left[...].reshape(512, 256).astype(BF16)
    rm = outgoing_right(got, 1 - lax.axis_index("core"), right)
    send[...] = outgoing_chunks(lm[...], rm, chunks).astype(BF16)


def outgoing_keep_kernel(got, lm, normed_t, proj_w, gate_w, out_w, keep, gate, w_t, out_t, right, chunks):
    keep[...] = outgoing_chunks(lm[...], outgoing_right(got, lax.axis_index("core"), right), chunks)
    gate[...] = sigmoid(dot(transposed(gate_w[0]), normed_t[...], ((1,), (0,))))
    w_t[...] = transposed_halved(proj_w[1])
    out_t[...] = transposed(out_w[0])


def incoming_left_kernel(got, lm, left):
    gather_groups(got[...].astype(F32).reshape(16, 8, 16, 128)[:, :, :8], left)
    lm[...] = left[...].reshape(512, 256).astype(BF16)


def incoming_near_kernel(got, lm, normed_t, gate_w, out_w, near, rm, gate, out_t, right):
    gather_groups(got[...].astype(F32).reshape(16, 8, 16, 128)[:, :, 8:], right)
    rm[...] = right[...].reshape(512, 256).astype(BF16)

    def store(c, t):
        near[:, c] = t

    scatter_groups(dot(lm[...], rm[...], ((0,), (0,))), store)
    gate[...] = sigmoid(dot(transposed(gate_w[1]), normed_t[...], ((1,), (0,))))
    out_t[...] = transposed(out_w[1])


def incoming_far_kernel(far, rm, near, send, chunks):
    core = lax.axis_index("core")
    chunks[:, core] = near[...]

    def store(c, t):
        chunks[:, 1 - core, c] = t

    scatter_groups(dot(far[...], rm[...], ((0,), (0,))), store)
    send[...] = chunks[...].reshape(1024, 128).astype(BF16)


def call(kernel, outs, scratch, flops=0):
    return pl.pallas_call(
        kernel,
        out_shape=[jax.ShapeDtypeStruct(shape, dtype) for shape, dtype in outs],
        scratch_shapes=[pltpu.VMEM(shape, dtype) for shape, dtype in scratch],
        compiler_params=pltpu.CompilerParams(vmem_limit_bytes=VMEM_LIMIT),
        cost_estimate=pl.CostEstimate(flops=flops, bytes_accessed=1 << 20, transcendentals=1 << 17) if flops else None,
    )


def body(pair, mask, proj_w, gate_w, out_w, ig, ib, mg, mb):
    def exchange(v):
        return lax.all_to_all(v, CHIPS, 0, 0, tiled=True)

    def swap(v):
        return lax.ppermute(v, "core", [(0, 1), (1, 0)])

    first = (pair, mask, proj_w, ig, ib, mg, mb)
    sent, pair_t, normed_t, m8, cols = pl.pallas_call(
        begin_kernel,
        in_specs=[pl.BlockSpec(memory_space=pl.ANY)] * 7,
        out_shape=[
            jax.ShapeDtypeStruct((2048, 128), BF16),
            jax.ShapeDtypeStruct((128, 1024), BF16),
            jax.ShapeDtypeStruct((128, 1024), BF16),
            jax.ShapeDtypeStruct((8, 128), F32),
            jax.ShapeDtypeStruct((128, 8), F32),
        ],
        scratch_shapes=[pltpu.VMEM(v.shape[1:] if v is proj_w else v.shape, v.dtype) for v in first]
        + [
            pltpu.VMEM(SCR, F32),
            pltpu.VMEM((8, 128), F32),
            pltpu.VMEM((512, 1024), F32),
            pltpu.SemaphoreType.DMA((10,)),
        ],
        compiler_params=pltpu.CompilerParams(vmem_limit_bytes=VMEM_LIMIT),
    )(*(pltpu.with_memory_space_constraint(v, pltpu.HBM) for v in first))
    wide = (128, 1024)
    square = (16, 4, 8, 256)
    half = (8, 4, 8, 256)
    got = exchange(sent).reshape(8, 2, 8, 16, 128)
    send, lm = call(
        outgoing_send_kernel,
        [((1024, 128), BF16), ((512, 256), BF16)],
        [(square, F32), (half, F32), ((16, 8, 8, 128), F32)],
    )(got)
    far = swap(send)
    keep, gate, w_t, out_t = call(
        outgoing_keep_kernel,
        [((1024, 128), F32), (wide, F32), ((512, 128), BF16), ((128, 128), BF16)],
        [(half, F32), ((16, 8, 8, 128), F32)],
        1 << 28,
    )(got, lm, normed_t, proj_w, gate_w, out_w)
    got = exchange((keep + far.astype(F32)).astype(BF16))
    sent, state_t, normed_t = call(
        middle_kernel,
        [((2048, 128), BF16), (wide, BF16), (wide, BF16)],
        [(TRI, F32), (SCR, F32), ((512, 1024), F32), (wide, F32), (wide, BF16)],
    )(got, pair_t, gate, m8, cols, w_t, out_t)
    got = exchange(sent).reshape(8, 2, 8, 16, 128)
    (lm,) = call(incoming_left_kernel, [((512, 256), BF16)], [(square, F32)])(got)
    far = swap(lm)
    near, rm, gate, out_t = call(
        incoming_near_kernel,
        [((8, 8, 8, 128), F32), ((512, 256), BF16), (wide, F32), ((128, 128), BF16)],
        [(square, F32)],
        1 << 28,
    )(got, lm, normed_t, gate_w, out_w)
    (send,) = call(incoming_far_kernel, [((1024, 128), BF16)], [((8, 2, 8, 8, 128), F32)])(far, rm, near)
    (out,) = call(
        end_kernel,
        [((4, 8, 32, 128), BF16)],
        [(TRI, F32), (wide, F32), (wide, BF16)],
    )(exchange(send), state_t, gate, cols, out_t)
    return out.reshape(32, 32, 128)


def solution(mesh):
    fine = Mesh(mesh.devices.reshape(4, 4, 2, 4, 2), ("zh", "x", "zl", "y", "core"))
    block = P(("zh", "x"), ("zl", "y", "core"))
    return jax.shard_map(
        body,
        mesh=fine,
        in_specs=(block, block, P(), P(), P(), P(), P(), P(), P()),
        out_specs=block,
        check_vma=False,
    )
```

```python
import jax
import jax.numpy as jnp
from jax import lax
from jax.experimental import pallas as pl
from jax.experimental.pallas import tpu as pltpu
from jax.sharding import Mesh
from jax.sharding import PartitionSpec as P

F32 = jnp.float32
BF16 = jnp.bfloat16
CHIPS = ("zh", "x", "zl", "y")
VMEM_LIMIT = 48 * 1024 * 1024
SCR = (2048 + 16, 128)
TRI = (1024 + 8, 128)


def dot(a, b, dims):
    return lax.dot_general(a, b, (dims, ((), ())), preferred_element_type=F32)


def sigmoid(v):
    return 0.5 * jnp.tanh(0.5 * v) + 0.5


def columns(gains, scr):
    for n, ref in enumerate(gains):
        scr[2 * n : 2 * n + 2, :] = ref[...]
    return scr[...].T


def norm_channels(v, gain, bias):
    mean = jnp.mean(v, axis=0, keepdims=True)
    centered = v - mean
    var = jnp.mean(centered * centered, axis=0, keepdims=True)
    return centered * lax.rsqrt(var + 1e-05) * gain + bias


def swap_groups(v):
    lane = lax.broadcasted_iota(jnp.int32, v[0].shape, v[0].ndim - 1)
    low = lane < 64
    even = (lane // 32) % 2 == 0
    axis = v[0].ndim - 1

    def exchange(a, b, keep, up, down):
        return jnp.where(keep, a, pltpu.roll(b, up, axis)), jnp.where(keep, pltpu.roll(a, down, axis), b)

    a0, a2 = exchange(v[0], v[2], low, 64, 64)
    a1, a3 = exchange(v[1], v[3], low, 64, 64)
    b0, b1 = exchange(a0, a1, even, 32, 96)
    b2, b3 = exchange(a2, a3, even, 32, 96)
    return [b0, b1, b2, b3]


def first_mask(mask):
    m = mask[...].astype(F32)
    return jnp.concatenate([m[8 * q : 8 * q + 8] for q in range(4)], axis=1)


def transposed(w):
    return w.astype(F32).T.astype(BF16)


def transposed_halved(w):
    t = w.astype(F32).T
    hid = t.shape[0] // 4
    row = lax.broadcasted_iota(jnp.int32, t.shape, 0)
    return jnp.where((row // hid) % 2 == 0, 0.5 * t, t).astype(BF16)


def lanes_of(a):
    return slice(128 * a, 128 * a + 128)


def gated(proj, mask, scr):
    hid = proj.shape[0] // 4
    for a in range(8):
        lanes = lanes_of(a)
        row = 0.5 * mask[a : a + 1, :]
        left = row * proj[hid : 2 * hid, lanes] * (jnp.tanh(proj[:hid, lanes]) + 1.0)
        right = row * proj[3 * hid :, lanes] * (jnp.tanh(proj[2 * hid : 3 * hid, lanes]) + 1.0)
        scr[pl.ds(a, hid, stride=16), :] = left
        scr[pl.ds(a + 8, hid, stride=16), :] = right


def begin_kernel(*refs):
    inputs, (sent, pair_t, normed_t, mask_out) = refs[:5], refs[5:9]
    local, (scr, gains, proj, sems) = refs[9:14], refs[14:]
    sources = (inputs[0], inputs[1], inputs[2].at[0], inputs[3], inputs[4])
    copies = [pltpu.make_async_copy(src, dst, sems.at[n]) for n, (src, dst) in enumerate(zip(sources, local))]
    for copy in copies:
        copy.start()
    for copy in copies:
        copy.wait()
    pair, mask, proj_w = local[:3]
    gains[...] = jnp.zeros_like(gains)
    col = columns(local[3:], gains)
    m8 = first_mask(mask)
    mask_out[...] = m8
    w_t = transposed_halved(proj_w[...])
    for a in range(8):
        block = jnp.concatenate([pair[8 * q + a] for q in range(4)], axis=0).astype(F32).T
        pair_t[:, lanes_of(a)] = block.astype(BF16)
        normed_t[:, lanes_of(a)] = norm_channels(block, col[:, 0:1], col[:, 2:3]).astype(BF16)
    proj[...] = dot(w_t, normed_t[...], ((1,), (0,)))
    gated(proj, m8, scr)
    sent[...] = scr[0:2048, :].astype(BF16)


def statistics(got, tri):
    v = got[...].astype(F32)
    tri[0:1024, :] = v
    v = v.reshape(8, 16, 8, 128)
    mean = jnp.mean(jnp.mean(v, axis=1), axis=0)
    centered = v - mean[None, None]
    return mean, lax.rsqrt(jnp.mean(jnp.mean(centered * centered, axis=1), axis=0) + 1e-05)


def norm_chunks(got, tri, gain, bias, out):
    mean, rstd = statistics(got, tri)
    chans = out.shape[0]
    for a in range(8):
        v = tri[pl.ds(a, chans, stride=8), :]
        out[:, lanes_of(a)] = ((v - mean[a : a + 1]) * rstd[a : a + 1] * gain + bias).astype(BF16)


def middle_kernel(got, pair_t, gate, mask, cols, w_t, out_t, sent, state_out, normed_out, tri, scr, proj, upd, tn):
    col = cols[...]
    norm_chunks(got, tri, col[:, 4:5], col[:, 6:7], tn)
    upd[...] = dot(out_t[...], tn[...], ((1,), (0,)))
    for a in range(8):
        lanes = lanes_of(a)
        state = (pair_t[:, lanes].astype(F32) + gate[:, lanes] * upd[:, lanes]).astype(BF16)
        state_out[:, lanes] = state
        normed_out[:, lanes] = norm_channels(state.astype(F32), col[:, 1:2], col[:, 3:4]).astype(BF16)
    proj[...] = dot(w_t[...], normed_out[...], ((1,), (0,)))
    gated(proj, mask[...], scr)
    sent[...] = scr[0:2048, :].astype(BF16)


def end_kernel(got, state_t, gate, cols, out_t, out, tri, upd, tn):
    col = cols[...]
    norm_chunks(got, tri, col[:, 5:6], col[:, 7:8], tn)
    upd[...] = dot(out_t[...], tn[...], ((1,), (0,)))
    for a in range(8):
        lanes = lanes_of(a)
        state = (state_t[:, lanes].astype(F32) + gate[:, lanes] * upd[:, lanes]).T.astype(BF16)
        out[:, a] = state.reshape(4, 32, 128)


def gather_groups(v, out):
    v = v.astype(F32)
    for h in range(2):
        for q, t in enumerate(swap_groups([v[:, 4 * h + g] for g in range(4)])):
            out[:, q, :, 128 * h : 128 * h + 128] = t


def scatter_groups(prod, store):
    v = prod.reshape(-1, 4, 8, 256)
    for h in range(2):
        lanes = slice(128 * h, 128 * h + 128)
        for g, t in enumerate(swap_groups([v[:, q, :, lanes] for q in range(4)])):
            store(4 * h + g, t)


def outgoing_chunks(lm, rm, chunks):
    prod = dot(lm, rm, ((1,), (1,)))

    def store(c, t):
        chunks[:, c] = t

    scatter_groups(prod, store)
    return chunks[...].reshape(1024, 128)


def outgoing_right(got, parity, right):
    gather_groups(got[:, parity].astype(F32)[:, :, 8:], right)
    return right[...].reshape(256, 256).astype(BF16)


def outgoing_send_kernel(got, send, lm, left, right, chunks):
    gather_groups(got[...].astype(F32).reshape(16, 8, 16, 128)[:, :, :8], left)
    lm[...] = left[...].reshape(512, 256).astype(BF16)
    rm = outgoing_right(got, 1 - lax.axis_index("core"), right)
    send[...] = outgoing_chunks(lm[...], rm, chunks).astype(BF16)


def outgoing_keep_kernel(
    got, lm, normed_t, proj_w, gate_w, out_w, ig, ib, mg, mb, keep, gate, w_t, out_t, cols, right, chunks, gains
):
    cols[...] = columns((ig, ib, mg, mb), gains)
    keep[...] = outgoing_chunks(lm[...], outgoing_right(got, lax.axis_index("core"), right), chunks)
    gate[...] = sigmoid(dot(transposed(gate_w[0]), normed_t[...], ((1,), (0,))))
    w_t[...] = transposed_halved(proj_w[1])
    out_t[...] = transposed(out_w[0])


def incoming_left_kernel(got, lm, left):
    gather_groups(got[...].astype(F32).reshape(16, 8, 16, 128)[:, :, :8], left)
    lm[...] = left[...].reshape(512, 256).astype(BF16)


def incoming_near_kernel(got, lm, normed_t, gate_w, out_w, near, rm, gate, out_t, right):
    gather_groups(got[...].astype(F32).reshape(16, 8, 16, 128)[:, :, 8:], right)
    rm[...] = right[...].reshape(512, 256).astype(BF16)

    def store(c, t):
        near[:, c] = t

    scatter_groups(dot(lm[...], rm[...], ((0,), (0,))), store)
    gate[...] = sigmoid(dot(transposed(gate_w[1]), normed_t[...], ((1,), (0,))))
    out_t[...] = transposed(out_w[1])


def incoming_far_kernel(far, rm, near, send, chunks):
    core = lax.axis_index("core")
    chunks[:, core] = near[...]

    def store(c, t):
        chunks[:, 1 - core, c] = t

    scatter_groups(dot(far[...], rm[...], ((0,), (0,))), store)
    send[...] = chunks[...].reshape(1024, 128).astype(BF16)


def call(kernel, outs, scratch, flops=0):
    return pl.pallas_call(
        kernel,
        out_shape=[jax.ShapeDtypeStruct(shape, dtype) for shape, dtype in outs],
        scratch_shapes=[pltpu.VMEM(shape, dtype) for shape, dtype in scratch],
        compiler_params=pltpu.CompilerParams(vmem_limit_bytes=VMEM_LIMIT),
        cost_estimate=pl.CostEstimate(flops=flops, bytes_accessed=1 << 20, transcendentals=1 << 17) if flops else None,
    )


def body(pair, mask, proj_w, gate_w, out_w, ig, ib, mg, mb):
    def exchange(v):
        return lax.all_to_all(v, CHIPS, 0, 0, tiled=True)

    def swap(v):
        return lax.ppermute(v, "core", [(0, 1), (1, 0)])

    first = (pair, mask, proj_w, ig, ib)
    sent, pair_t, normed_t, m8 = pl.pallas_call(
        begin_kernel,
        in_specs=[pl.BlockSpec(memory_space=pl.ANY)] * 5,
        out_shape=[
            jax.ShapeDtypeStruct((2048, 128), BF16),
            jax.ShapeDtypeStruct((128, 1024), BF16),
            jax.ShapeDtypeStruct((128, 1024), BF16),
            jax.ShapeDtypeStruct((8, 128), F32),
        ],
        scratch_shapes=[pltpu.VMEM(v.shape[1:] if v is proj_w else v.shape, v.dtype) for v in first]
        + [
            pltpu.VMEM(SCR, F32),
            pltpu.VMEM((8, 128), F32),
            pltpu.VMEM((512, 1024), F32),
            pltpu.SemaphoreType.DMA((5,)),
        ],
        compiler_params=pltpu.CompilerParams(vmem_limit_bytes=VMEM_LIMIT),
    )(*(pltpu.with_memory_space_constraint(v, pltpu.HBM) for v in first))
    wide = (128, 1024)
    square = (16, 4, 8, 256)
    half = (8, 4, 8, 256)
    got = exchange(sent).reshape(8, 2, 8, 16, 128)
    send, lm = call(
        outgoing_send_kernel,
        [((1024, 128), BF16), ((512, 256), BF16)],
        [(square, F32), (half, F32), ((16, 8, 8, 128), F32)],
    )(got)
    far = swap(send)
    keep, gate, w_t, out_t, cols = call(
        outgoing_keep_kernel,
        [((1024, 128), F32), (wide, F32), ((512, 128), BF16), ((128, 128), BF16), ((128, 8), F32)],
        [(half, F32), ((16, 8, 8, 128), F32), ((8, 128), F32)],
        1 << 28,
    )(got, lm, normed_t, proj_w, gate_w, out_w, ig, ib, mg, mb)
    got = exchange((keep + far.astype(F32)).astype(BF16))
    sent, state_t, normed_t = call(
        middle_kernel,
        [((2048, 128), BF16), (wide, BF16), (wide, BF16)],
        [(TRI, F32), (SCR, F32), ((512, 1024), F32), (wide, F32), (wide, BF16)],
    )(got, pair_t, gate, m8, cols, w_t, out_t)
    got = exchange(sent).reshape(8, 2, 8, 16, 128)
    (lm,) = call(incoming_left_kernel, [((512, 256), BF16)], [(square, F32)])(got)
    far = swap(lm)
    near, rm, gate, out_t = call(
        incoming_near_kernel,
        [((8, 8, 8, 128), F32), ((512, 256), BF16), (wide, F32), ((128, 128), BF16)],
        [(square, F32)],
        1 << 28,
    )(got, lm, normed_t, gate_w, out_w)
    (send,) = call(incoming_far_kernel, [((1024, 128), BF16)], [((8, 2, 8, 8, 128), F32)])(far, rm, near)
    (out,) = call(
        end_kernel,
        [((4, 8, 32, 128), BF16)],
        [(TRI, F32), (wide, F32), (wide, BF16)],
    )(exchange(send), state_t, gate, cols, out_t)
    return out.reshape(32, 32, 128)


def solution(mesh):
    fine = Mesh(mesh.devices.reshape(4, 4, 2, 4, 2), ("zh", "x", "zl", "y", "core"))
    block = P(("zh", "x"), ("zl", "y", "core"))
    return jax.shard_map(
        body,
        mesh=fine,
        in_specs=(block, block, P(), P(), P(), P(), P(), P(), P()),
        out_specs=block,
        check_vma=False,
    )
```

```python
import jax
import jax.numpy as jnp
from jax import lax
from jax.experimental import pallas as pl
from jax.experimental.pallas import tpu as pltpu
from jax.sharding import Mesh
from jax.sharding import PartitionSpec as P

F32 = jnp.float32
BF16 = jnp.bfloat16
CHIPS = ("zh", "x", "zl", "y")
VMEM_LIMIT = 48 * 1024 * 1024
SCR = (2048 + 16, 128)
TRI = (1024 + 8, 128)


def dot(a, b, dims):
    return lax.dot_general(a, b, (dims, ((), ())), preferred_element_type=F32)


def sigmoid(v):
    return 0.5 * jnp.tanh(0.5 * v) + 0.5


def columns(gains, scr):
    for n, ref in enumerate(gains):
        scr[2 * n : 2 * n + 2, :] = ref[...]
    return scr[...].T


def norm_channels(v, gain, bias):
    mean = jnp.mean(v, axis=0, keepdims=True)
    centered = v - mean
    var = jnp.mean(centered * centered, axis=0, keepdims=True)
    return centered * lax.rsqrt(var + 1e-05) * gain + bias


def swap_groups(v):
    lane = lax.broadcasted_iota(jnp.int32, v[0].shape, v[0].ndim - 1)
    low = lane < 64
    even = (lane // 32) % 2 == 0
    axis = v[0].ndim - 1

    def exchange(a, b, keep, up, down):
        return jnp.where(keep, a, pltpu.roll(b, up, axis)), jnp.where(keep, pltpu.roll(a, down, axis), b)

    a0, a2 = exchange(v[0], v[2], low, 64, 64)
    a1, a3 = exchange(v[1], v[3], low, 64, 64)
    b0, b1 = exchange(a0, a1, even, 32, 96)
    b2, b3 = exchange(a2, a3, even, 32, 96)
    return [b0, b1, b2, b3]


def first_mask(mask):
    m = mask[...].astype(F32)
    return jnp.concatenate([m[8 * q : 8 * q + 8] for q in range(4)], axis=1)


def transposed(w):
    return w.astype(F32).T.astype(BF16)


def transposed_halved(w):
    t = w.astype(F32).T
    hid = t.shape[0] // 4
    row = lax.broadcasted_iota(jnp.int32, t.shape, 0)
    return jnp.where((row // hid) % 2 == 0, 0.5 * t, t).astype(BF16)


def lanes_of(a):
    return slice(128 * a, 128 * a + 128)


def gated(proj, mask, scr):
    hid = proj.shape[0] // 4
    for a in range(8):
        lanes = lanes_of(a)
        row = 0.5 * mask[a : a + 1, :]
        left = row * proj[hid : 2 * hid, lanes] * (jnp.tanh(proj[:hid, lanes]) + 1.0)
        right = row * proj[3 * hid :, lanes] * (jnp.tanh(proj[2 * hid : 3 * hid, lanes]) + 1.0)
        scr[pl.ds(a, hid, stride=16), :] = left
        scr[pl.ds(a + 8, hid, stride=16), :] = right


def begin_kernel(*refs):
    inputs, (sent, pair_t, normed_t, mask_out, cols) = refs[:7], refs[7:12]
    local, (scr, gains, proj, sems) = refs[12:19], refs[19:]
    parts = [(inputs[0].at[8 * n : 8 * n + 8], local[0].at[8 * n : 8 * n + 8]) for n in range(4)]
    parts += [(inputs[2].at[0], local[2]), (inputs[1], local[1])] + list(zip(inputs[3:], local[3:]))
    copies = [pltpu.make_async_copy(src, dst, sems.at[n]) for n, (src, dst) in enumerate(parts)]
    for copy in copies:
        copy.start()
    for copy in copies:
        copy.wait()
    pair, mask, proj_w = local[:3]
    col = columns(local[3:], gains)
    cols[...] = col
    m8 = first_mask(mask)
    mask_out[...] = m8
    w_t = transposed_halved(proj_w[...])
    for a in range(8):
        block = jnp.concatenate([pair[8 * q + a] for q in range(4)], axis=0).astype(F32).T
        pair_t[:, lanes_of(a)] = block.astype(BF16)
        normed_t[:, lanes_of(a)] = norm_channels(block, col[:, 0:1], col[:, 2:3]).astype(BF16)
    proj[...] = dot(w_t, normed_t[...], ((1,), (0,)))
    gated(proj, m8, scr)
    sent[...] = scr[0:2048, :].astype(BF16)


def statistics(got, tri):
    v = got[...].astype(F32)
    tri[0:1024, :] = v
    v = v.reshape(8, 16, 8, 128)
    mean = jnp.mean(jnp.mean(v, axis=1), axis=0)
    centered = v - mean[None, None]
    return mean, lax.rsqrt(jnp.mean(jnp.mean(centered * centered, axis=1), axis=0) + 1e-05)


def norm_chunks(got, tri, gain, bias, out):
    mean, rstd = statistics(got, tri)
    chans = out.shape[0]
    for a in range(8):
        v = tri[pl.ds(a, chans, stride=8), :]
        out[:, lanes_of(a)] = ((v - mean[a : a + 1]) * rstd[a : a + 1] * gain + bias).astype(BF16)


def middle_kernel(got, pair_t, gate, mask, cols, w_t, out_t, sent, state_out, normed_out, tri, scr, proj, upd, tn):
    col = cols[...]
    norm_chunks(got, tri, col[:, 4:5], col[:, 6:7], tn)
    upd[...] = dot(out_t[...], tn[...], ((1,), (0,)))
    for a in range(8):
        lanes = lanes_of(a)
        state = (pair_t[:, lanes].astype(F32) + gate[:, lanes].astype(F32) * upd[:, lanes]).astype(BF16)
        state_out[:, lanes] = state
        normed_out[:, lanes] = norm_channels(state.astype(F32), col[:, 1:2], col[:, 3:4]).astype(BF16)
    proj[...] = dot(w_t[...], normed_out[...], ((1,), (0,)))
    gated(proj, mask[...], scr)
    sent[...] = scr[0:2048, :].astype(BF16)


def end_kernel(got, state_t, gate, cols, out_t, out, tri, upd, tn):
    col = cols[...]
    norm_chunks(got, tri, col[:, 5:6], col[:, 7:8], tn)
    upd[...] = dot(out_t[...], tn[...], ((1,), (0,)))
    for a in range(8):
        lanes = lanes_of(a)
        state = (state_t[:, lanes].astype(F32) + gate[:, lanes].astype(F32) * upd[:, lanes]).T.astype(BF16)
        out[:, a] = state.reshape(4, 32, 128)


def gather_groups(v, out):
    v = v.astype(F32)
    for h in range(2):
        for q, t in enumerate(swap_groups([v[:, 4 * h + g] for g in range(4)])):
            out[:, q, :, 128 * h : 128 * h + 128] = t


def scatter_groups(prod, store):
    v = prod.reshape(-1, 4, 8, 256)
    for h in range(2):
        lanes = slice(128 * h, 128 * h + 128)
        for g, t in enumerate(swap_groups([v[:, q, :, lanes] for q in range(4)])):
            store(4 * h + g, t)


def outgoing_chunks(lm, rm, chunks):
    prod = dot(lm, rm, ((1,), (1,)))

    def store(c, t):
        chunks[:, c] = t

    scatter_groups(prod, store)
    return chunks[...].reshape(1024, 128)


def outgoing_right(got, parity, right):
    gather_groups(got[:, parity].astype(F32)[:, :, 8:], right)
    return right[...].reshape(256, 256).astype(BF16)


def outgoing_send_kernel(got, send, lm, left, right, chunks):
    gather_groups(got[...].astype(F32).reshape(16, 8, 16, 128)[:, :, :8], left)
    lm[...] = left[...].reshape(512, 256).astype(BF16)
    rm = outgoing_right(got, 1 - lax.axis_index("core"), right)
    send[...] = outgoing_chunks(lm[...], rm, chunks).astype(BF16)


def outgoing_keep_kernel(got, lm, normed_t, proj_w, gate_w, out_w, keep, gate, w_t, out_t, right, chunks):
    keep[...] = outgoing_chunks(lm[...], outgoing_right(got, lax.axis_index("core"), right), chunks)
    gate[...] = sigmoid(dot(transposed(gate_w[0]), normed_t[...], ((1,), (0,)))).astype(BF16)
    w_t[...] = transposed_halved(proj_w[1])
    out_t[...] = transposed(out_w[0])


def incoming_left_kernel(got, lm, left):
    gather_groups(got[...].astype(F32).reshape(16, 8, 16, 128)[:, :, :8], left)
    lm[...] = left[...].reshape(512, 256).astype(BF16)


def incoming_near_kernel(got, lm, normed_t, gate_w, out_w, near, rm, gate, out_t, right):
    gather_groups(got[...].astype(F32).reshape(16, 8, 16, 128)[:, :, 8:], right)
    rm[...] = right[...].reshape(512, 256).astype(BF16)

    def store(c, t):
        near[:, c] = t

    scatter_groups(dot(lm[...], rm[...], ((0,), (0,))), store)
    gate[...] = sigmoid(dot(transposed(gate_w[1]), normed_t[...], ((1,), (0,)))).astype(BF16)
    out_t[...] = transposed(out_w[1])


def incoming_far_kernel(far, rm, near, send, chunks):
    core = lax.axis_index("core")
    chunks[:, core] = near[...]

    def store(c, t):
        chunks[:, 1 - core, c] = t

    scatter_groups(dot(far[...], rm[...], ((0,), (0,))), store)
    send[...] = chunks[...].reshape(1024, 128).astype(BF16)


def call(kernel, outs, scratch, flops=0):
    return pl.pallas_call(
        kernel,
        out_shape=[jax.ShapeDtypeStruct(shape, dtype) for shape, dtype in outs],
        scratch_shapes=[pltpu.VMEM(shape, dtype) for shape, dtype in scratch],
        compiler_params=pltpu.CompilerParams(vmem_limit_bytes=VMEM_LIMIT),
        cost_estimate=pl.CostEstimate(flops=flops, bytes_accessed=1 << 20, transcendentals=1 << 17) if flops else None,
    )


def body(pair, mask, proj_w, gate_w, out_w, ig, ib, mg, mb):
    def exchange(v):
        return lax.all_to_all(v, CHIPS, 0, 0, tiled=True)

    def swap(v):
        return lax.ppermute(v, "core", [(0, 1), (1, 0)])

    first = (pair, mask, proj_w, ig, ib, mg, mb)
    sent, pair_t, normed_t, m8, cols = pl.pallas_call(
        begin_kernel,
        in_specs=[pl.BlockSpec(memory_space=pl.ANY)] * 7,
        out_shape=[
            jax.ShapeDtypeStruct((2048, 128), BF16),
            jax.ShapeDtypeStruct((128, 1024), BF16),
            jax.ShapeDtypeStruct((128, 1024), BF16),
            jax.ShapeDtypeStruct((8, 128), F32),
            jax.ShapeDtypeStruct((128, 8), F32),
        ],
        scratch_shapes=[pltpu.VMEM(v.shape[1:] if v is proj_w else v.shape, v.dtype) for v in first]
        + [
            pltpu.VMEM(SCR, F32),
            pltpu.VMEM((8, 128), F32),
            pltpu.VMEM((512, 1024), F32),
            pltpu.SemaphoreType.DMA((10,)),
        ],
        compiler_params=pltpu.CompilerParams(vmem_limit_bytes=VMEM_LIMIT),
    )(*(pltpu.with_memory_space_constraint(v, pltpu.HBM) for v in first))
    wide = (128, 1024)
    square = (16, 4, 8, 256)
    half = (8, 4, 8, 256)
    got = exchange(sent).reshape(8, 2, 8, 16, 128)
    send, lm = call(
        outgoing_send_kernel,
        [((1024, 128), BF16), ((512, 256), BF16)],
        [(square, F32), (half, F32), ((16, 8, 8, 128), F32)],
    )(got)
    far = swap(send)
    keep, gate, w_t, out_t = call(
        outgoing_keep_kernel,
        [((1024, 128), F32), (wide, BF16), ((512, 128), BF16), ((128, 128), BF16)],
        [(half, F32), ((16, 8, 8, 128), F32)],
        1 << 28,
    )(got, lm, normed_t, proj_w, gate_w, out_w)
    got = exchange((keep + far.astype(F32)).astype(BF16))
    sent, state_t, normed_t = call(
        middle_kernel,
        [((2048, 128), BF16), (wide, BF16), (wide, BF16)],
        [(TRI, F32), (SCR, F32), ((512, 1024), F32), (wide, F32), (wide, BF16)],
    )(got, pair_t, gate, m8, cols, w_t, out_t)
    got = exchange(sent).reshape(8, 2, 8, 16, 128)
    (lm,) = call(incoming_left_kernel, [((512, 256), BF16)], [(square, F32)])(got)
    far = swap(lm)
    near, rm, gate, out_t = call(
        incoming_near_kernel,
        [((8, 8, 8, 128), F32), ((512, 256), BF16), (wide, BF16), ((128, 128), BF16)],
        [(square, F32)],
        1 << 28,
    )(got, lm, normed_t, gate_w, out_w)
    (send,) = call(incoming_far_kernel, [((1024, 128), BF16)], [((8, 2, 8, 8, 128), F32)])(far, rm, near)
    (out,) = call(
        end_kernel,
        [((4, 8, 32, 128), BF16)],
        [(TRI, F32), (wide, F32), (wide, BF16)],
    )(exchange(send), state_t, gate, cols, out_t)
    return out.reshape(32, 32, 128)


def solution(mesh):
    fine = Mesh(mesh.devices.reshape(4, 4, 2, 4, 2), ("zh", "x", "zl", "y", "core"))
    block = P(("zh", "x"), ("zl", "y", "core"))
    return jax.shard_map(
        body,
        mesh=fine,
        in_specs=(block, block, P(), P(), P(), P(), P(), P(), P()),
        out_specs=block,
        check_vma=False,
    )
```
